256 devices in a mesh: ctx: 32 (over x, y, core), kvh: 8 (over z).
Axes of the slice: x: 4, y: 4, z: 8, core: 2. Of those that a mesh axis runs over, the one named last changes fastest.
Arguments:
- queries: bfloat16 [256, 128, 128], P('ctx', 'kvh'), may hold values from -120 to 120
- key_cache: bfloat16 [131072, 8, 128], P('ctx', 'kvh'), may hold values from -5 to 5
- value_cache: bfloat16 [131072, 8, 128], P('ctx', 'kvh'), may hold values from -6 to 6
- block_lengths: int32 [512], replicated, may hold values from 1 to 256, 98304 in all
- block_home: int32 [512], replicated, may hold values from 0 to 511, as said below
- stretch_start: int32 [1], replicated, may hold values from 256 to 98048
- out_weight: bfloat16 [16384, 16384], P('kvh', 'ctx'), may hold values from -0.046875 to 0.046875
Outputs:
- attention: bfloat16 [256, 128, 128], P('ctx', 'kvh')
- projected: bfloat16 [256, 16384], P('kvh', 'ctx')
The draws below stay inside these ranges and needn't reach their ends.
Inputs may be any that keep to these rules, and one draw needn't show every extreme that they name: `block_lengths`: the lengths sum to 98304. `block_home`: a permutation; device d of ctx stores pages d * 16 onward; the logical pages of each aligned run of twice as many pages as ctx has devices go two to a device, one from each half of the run at mirrored places.
All inputs are finite; a program needn't handle non-finite values.
Results may differ from the reference program's by a relative error of at most 0.019.
Values may be sent and summed in bfloat16 or wider, within the bound.
A program may use at most 64 MiB of HBM per device.

```python
import math
import jax
import jax.numpy as jnp
import numpy as np
from jax import lax

HEADS = 128
KVH = 8
HD = 128
D = 16384
CTX_DEV = 4096
PAGE = 256
QTOK = 256
SLOTS = 131072
PAGES = 512
FILLED = 98304
N_CTX = 32


def mirrored_home(key):
    key = jax.random.fold_in(key, 101)
    local_pages = CTX_DEV // PAGE
    rounds = local_pages // 2
    orders = jax.vmap(lambda round_key: jax.random.permutation(round_key, N_CTX))(jax.random.split(key, rounds))
    logical = jnp.arange(PAGES, dtype=jnp.int32)
    span_pages = 2 * N_CTX
    round_of = logical // span_pages
    position_in_round = logical % span_pages
    mirrored = jnp.minimum(position_in_round, span_pages - 1 - position_in_round)
    upper_half = (position_in_round >= N_CTX).astype(jnp.int32)
    owners = orders[round_of, mirrored].astype(jnp.int32)
    return (owners * local_pages + 2 * round_of + upper_half).astype(jnp.int32)


def draw_block_home(key, part):
    return mirrored_home(key)


def draw_key_cache(key, part):
    own_key = jax.random.fold_in(key, 3)
    keys_drawn = jnp.clip(jax.random.normal(own_key, (SLOTS, KVH, HD), jnp.float32), -5.0, 5.0)
    return keys_drawn.astype(jnp.bfloat16)


def draw_queries(key, part):
    own_key = jax.random.fold_in(key, 4)
    drawn_values = jnp.clip(3.0 * jax.random.normal(own_key, (QTOK, HEADS, HD), jnp.float32), -18.0, 18.0)
    return drawn_values.astype(jnp.bfloat16)


def level_of(stream_key, dims, shards, smallest, high):
    factor_of, own = 1.0, jax.random.fold_in(stream_key, 6)
    for position, shards_of in shards:
        draws = jnp.exp(jax.random.uniform(jax.random.fold_in(own, position), (shards_of,), jnp.float32, smallest / len(shards), high / len(shards)))
        factor_of = factor_of * jnp.repeat(draws, dims[position] // shards_of).reshape([-1 if axis == position else 1 for axis in range(len(dims))])
    return factor_of


def split_up(count, total, limit, slope):
    loads = [(1 << 20) // math.isqrt(grade ** slope) + 1 for grade in range(2, count + 1)]
    spare, given = total - limit - (count - 1), [1] * (count - 1)
    while spare > 0:
        movable = [i for i in range(count - 1) if given[i] < limit]
        mass, left = sum([loads[i] for i in movable]), spare
        for i in movable:
            extra = min(limit - given[i], max(1, left * loads[i] // mass), spare)
            given[i] = given[i] + extra
            spare = spare - extra
    return np.array([limit] + given)


def uneven(key, amount, total, reach, slope):
    if amount == 2:
        one = jax.random.randint(key, (), max(1, total - reach), min(reach, total - 1) + 1)
        return jnp.stack([one, total - one])
    tallies = jnp.asarray(split_up(amount, total, reach, slope), jnp.int32)
    couples = (amount - 1) // 2
    giver, sink = tallies[1:1 + 2 * couples:2], tallies[2:2 + 2 * couples:2]
    slack = jnp.minimum(giver - 1, reach - sink)
    shifted = jax.random.randint(jax.random.fold_in(key, 1), (couples,), 0, 1 << 20) % (slack + 1)
    tallies = tallies.at[1:1 + 2 * couples:2].set(giver - shifted).at[2:2 + 2 * couples:2].set(sink + shifted)
    return tallies[jax.random.permutation(jax.random.fold_in(key, 2), amount)]


def centred(rng, extent, deviation, most, cuts=(), held_as=jnp.bfloat16):
    entries = deviation * jax.random.normal(rng, extent, jnp.float32)
    if cuts:
        entries = entries * level_of(rng, extent, cuts, -0.22, 0.18)
    return jnp.clip(entries, -most, most).astype(held_as)


def setup_inputs(seed: int = 0) -> dict:
    streams_of = jax.random.split(jax.random.key(seed), 8)
    queries = draw_queries(jax.random.fold_in(streams_of[7], 71), 0)
    key_cache = draw_key_cache(jax.random.fold_in(streams_of[7], 71), 0)
    value_cache = centred(streams_of[2], (SLOTS, KVH, HD), 1.0, 6.0, ((0, 32), (1, 8)))
    block_lengths = uneven(streams_of[3], PAGES, FILLED, PAGE, 0).astype(jnp.int32)
    block_home = draw_block_home(jax.random.fold_in(streams_of[7], 71), 0)
    stretch_start = jax.random.randint(streams_of[5], (1,), PAGE, FILLED - QTOK + 1).astype(jnp.int32)
    out_weight = centred(streams_of[6], (D, D), D ** -0.5, 0.046875, ((0, 8), (1, 32)))
    return {"queries": queries, "key_cache": key_cache, "value_cache": value_cache, "block_lengths": block_lengths, "block_home": block_home, "stretch_start": stretch_start, "out_weight": out_weight}


MASKED_SCORE = -1.0e30
FAR_POSITION = 1 << 30


def reference(queries, key_cache, value_cache, block_lengths, block_home, stretch_start, out_weight):
    page_count = block_lengths.shape[0]
    starts_all = jnp.cumsum(block_lengths) - block_lengths
    logical = jnp.zeros((page_count,), jnp.int32).at[block_home].set(jnp.arange(page_count, dtype=jnp.int32))
    offsets = starts_all[logical]
    filled = block_lengths[logical]
    slot_index = jnp.arange(PAGE, dtype=jnp.int32)
    key_pos = jnp.where(slot_index[None, :] < filled[:, None], offsets[:, None] + slot_index[None, :], FAR_POSITION)
    query_pos = stretch_start[0] + jnp.arange(QTOK, dtype=jnp.int32)
    group_size = HEADS // KVH
    grouped = queries.astype(jnp.float32).reshape(QTOK, KVH, group_size, HD)
    key_pages = key_cache.reshape(page_count, PAGE, KVH, HD)
    value_pages = value_cache.reshape(page_count, PAGE, KVH, HD)
    scaling = HD ** -0.5

    def visit_page(running, page_data):
        key_block, value_block, pos_block = page_data
        visible = pos_block[None, :] <= query_pos[:, None]
        visible_mask = visible[:, None, None, :]
        scores = jnp.einsum('tkgd,pkd->tkgp', grouped, key_block.astype(jnp.float32)) * scaling
        page_peaks = jnp.max(jnp.where(visible_mask, scores, MASKED_SCORE), axis=-1)
        weights = jnp.where(visible_mask, jnp.exp(scores - page_peaks[..., None]), 0.0)
        page_totals = jnp.sum(weights, axis=-1)
        rounded = lax.optimization_barrier(weights.astype(jnp.bfloat16)).astype(jnp.float32)
        page_mixed = jnp.einsum('tkgp,pkd->tkgd', rounded, value_block.astype(jnp.float32))
        running_top, totals, accumulated = running
        new_top = jnp.maximum(running_top, page_peaks)
        carried_scale = jnp.exp(running_top - new_top)
        fresh_scale = jnp.exp(page_peaks - new_top)
        totals = totals * carried_scale + page_totals * fresh_scale
        accumulated = accumulated * carried_scale[..., None] + page_mixed * fresh_scale[..., None]
        return (new_top, totals, accumulated), None

    initial = (jnp.full((QTOK, KVH, group_size), MASKED_SCORE, jnp.float32),
               jnp.zeros((QTOK, KVH, group_size), jnp.float32),
               jnp.zeros((QTOK, KVH, group_size, HD), jnp.float32))
    (running_top, totals, accumulated), _ = lax.scan(visit_page, initial, (key_pages, value_pages, key_pos))
    attention = (accumulated / totals[..., None]).astype(jnp.bfloat16).reshape(QTOK, HEADS, HD)
    projected = jnp.dot(attention.reshape(QTOK, HEADS * HD), out_weight, preferred_element_type=jnp.float32).astype(jnp.bfloat16)
    return attention, projected
```

```python
import functools
import math

import jax
import jax.numpy as jnp
from jax import lax
from jax.experimental import pallas as pl
from jax.experimental.pallas import tpu as pltpu
from jax.sharding import PartitionSpec as P

HD = 128
PAGE = 256
NEG = -1e30
FAR = 1 << 30
LOG2E_SCALE = math.log2(math.e) / math.sqrt(HD)
F32 = jnp.float32
BF16 = jnp.bfloat16
VMEM_LIMIT = 56 * 1024 * 1024


def greet(devices):
    barrier = pltpu.get_barrier_semaphore()
    count = 0
    for first, number, device_of in devices:
        count += number

        def body(k, _, device_of=device_of):
            pl.semaphore_signal(
                barrier, inc=1, device_id=device_of(k), device_id_type=pl.DeviceIdType.MESH
            )
            return 0

        lax.fori_loop(first, first + number, body, 0)
    pl.semaphore_wait(barrier, count)


def remote(src, dst, send, recv, device):
    return pltpu.make_async_remote_copy(
        src_ref=src,
        dst_ref=dst,
        send_sem=send,
        recv_sem=recv,
        device_id=device,
        device_id_type=pl.DeviceIdType.MESH,
    )


def loop(start, stop, body):
    def step(k, _):
        body(k)
        return 0

    lax.fori_loop(start, stop, step, 0)


def spread(chips, chip, core, at, own, send, recv, sib_send, sib_recv):
    other = {"ctx": chip * 2 + 1 - core}

    def start(k):
        peer = lax.rem(chip + k, chips)
        remote(own, at(chip, core), send.at[k], recv.at[chip], {"ctx": peer * 2 + core}).start()

    loop(1, chips, start)
    remote(own, at(chip, core), sib_send.at[chip], sib_recv.at[chip], other).start()

    def forward(k):
        source = lax.rem(chip + k, chips)
        here = at(source, core)
        remote(own, here, send.at[k], recv.at[source], {"ctx": source * 2 + core}).wait_recv()
        remote(here, here, sib_send.at[source], sib_recv.at[source], other).start()

    loop(1, chips, forward)


def spread_finish(chips, chip, core, at, own, send, recv, sib_send, sib_recv):
    other = {"ctx": chip * 2 + 1 - core}

    def finish(source):
        there = at(source, 1 - core)
        remote(own, there, sib_send.at[source], sib_recv.at[source], other).wait_recv()

    loop(0, chips, finish)

    def sent(k):
        peer = lax.rem(chip + k, chips)
        remote(own, at(chip, core), send.at[k], recv.at[chip], {"ctx": peer * 2 + core}).wait_send()

    loop(1, chips, sent)

    def passed(source):
        here = at(source, core)
        remote(here, here, sib_send.at[source], sib_recv.at[source], other).wait_send()

    loop(0, chips, passed)


def gather_kernel(
    chips, q_ref, len_ref, home_ref, qall_ref, meta_ref, mine, send, recv, sib_send, sib_recv, own_sem
):
    ctx = lax.axis_index("ctx")
    chip, core = ctx // 2, lax.rem(ctx, 2)
    tokens, heads = q_ref.shape[0], q_ref.shape[1]
    half = heads // 2
    wide = q_ref[...].astype(F32)
    for part in range(2):
        rows = wide[:, part * half : (part + 1) * half, :].reshape(tokens * half, HD)
        mine[part] = rows.astype(BF16)
    greet(
        [
            (1, chips - 1, lambda k: {"ctx": lax.rem(chip + k, chips) * 2 + core}),
            (0, 1, lambda k: {"ctx": chip * 2 + 1 - core}),
        ]
    )
    def at(p, c):
        return qall_ref.at[p, :, c]

    own = pltpu.make_async_copy(mine, at(chip, core), own_sem)
    own.start()
    spread(chips, chip, core, at, mine, send, recv, sib_send, sib_recv)

    pages, blocks = meta_ref.shape[0], home_ref.shape[1]
    lengths = len_ref[...].astype(F32)
    stored = ctx * pages + lax.broadcasted_iota(jnp.int32, (pages, blocks), 0)
    logical = lax.broadcasted_iota(jnp.int32, (pages, blocks), 1).astype(F32)
    match = home_ref[...] == stored
    place = jnp.sum(jnp.where(match, logical, 0.0), axis=1, keepdims=True)
    filled = jnp.sum(jnp.where(match, lengths, 0.0), axis=1, keepdims=True)
    begin = jnp.sum(jnp.where(logical < place, lengths, 0.0), axis=1, keepdims=True)
    lane = lax.broadcasted_iota(jnp.int32, (pages, 128), 1)
    meta = jnp.where(lane == 0, begin, jnp.where(lane == 1, filled, 0.0))
    meta_ref[...] = meta.astype(jnp.int32)

    own.wait()
    spread_finish(chips, chip, core, at, mine, send, recv, sib_send, sib_recv)


def gather_queries(mesh, queries, block_lengths, block_home, pages):
    chips = mesh.shape["ctx"] // 2
    tokens, heads, _ = queries.shape
    rows = tokens * heads // 2
    dma = pltpu.SemaphoreType.DMA((chips,))
    vmem = pl.BlockSpec(memory_space=pltpu.VMEM)
    return pl.pallas_call(
        functools.partial(gather_kernel, chips),
        out_shape=(
            jax.ShapeDtypeStruct((chips, 2, 2, rows, HD), BF16),
            jax.ShapeDtypeStruct((pages, 128), jnp.int32),
        ),
        in_specs=[vmem] * 3,
        out_specs=(pl.BlockSpec(memory_space=pl.ANY), vmem),
        scratch_shapes=[pltpu.VMEM((2, rows, HD), BF16), dma, dma, dma, dma, pltpu.SemaphoreType.DMA],
        compiler_params=pltpu.CompilerParams(collective_id=0, has_side_effects=True),
        name="gather_queries",
    )(queries, block_lengths.reshape(1, -1), block_home.reshape(1, -1))


def attend_kernel(
    tile, chunk, tokens_here, half_heads,
    meta_ref, start_ref, q_ref, k_ref, v_ref, o_ref, stat_ref,
    kc, vc, scores, peaks, tops, sums, tail, base_ref,
):
    pages = meta_ref.shape[0]
    rows_all = q_ref.shape[0]
    tiles = rows_all // tile
    tokens = rows_all // (2 * half_heads)
    chip_rows = 4 * tokens_here * half_heads
    first = start_ref[0]
    last = first + tokens - 1
    slot = lax.broadcasted_iota(jnp.int32, (PAGE, HD), 0)

    def visit(page, used, masked):
        begin, filled = meta_ref[page, 0], meta_ref[page, 1]
        partly = begin + filled - 1 > first
        seen = begin <= last
        take = jnp.logical_and(seen, partly) if masked else jnp.logical_not(partly)

        @pl.when(take)
        def _():
            base_ref[page] = used
            source = pl.ds(pl.multiple_of(page * PAGE, PAGE), PAGE)
            target = pl.ds(pl.multiple_of(used, 16), PAGE)
            keys = k_ref[source, :].astype(F32)
            live = slot < filled
            lead = jnp.broadcast_to(keys[0:1, :], (PAGE, HD))
            kc[target, :] = jnp.where(live, keys, lead).astype(BF16)
            tail[...] = lead[0:16, :].astype(BF16)
            values = v_ref[source, :].astype(F32)
            vc[target, 0:HD] = jnp.where(live, values, 0.0).astype(BF16)
            vc[target, HD : 2 * HD] = jnp.where(live, 1.0, 0.0).astype(BF16)

        if not masked:

            @pl.when(jnp.logical_not(take))
            def _():
                base_ref[page] = FAR

        return used + jnp.where(take, (filled + 15) // 16 * 16, 0)

    tail[...] = jnp.zeros_like(tail)
    plain = lax.fori_loop(0, pages, lambda p, u: visit(p, u, False), jnp.int32(0))
    used = lax.fori_loop(0, pages, lambda p, u: visit(p, u, True), plain)
    for piece in range(chunk // 16):
        target = pl.ds(pl.multiple_of(used + piece * 16, 16), 16)
        kc[target, :] = tail[...]
        vc[target, :] = jnp.zeros((16, 2 * HD), BF16)
    chunks = (used + chunk - 1) // chunk
    clear = jnp.where(used > plain, plain // chunk, chunks)

    def score(tile_index, buffer, position, masked):
        q = q_ref[pl.ds(pl.multiple_of(tile_index * tile, tile), tile), :]
        keys = kc[pl.ds(pl.multiple_of(position * chunk, chunk), chunk), :]
        s = lax.dot_general(q, keys, (((1,), (1,)), ((), ())), preferred_element_type=F32)
        if masked:
            index = position * chunk + lax.broadcasted_iota(jnp.int32, (1, chunk), 1)

            def mark(page, key_pos):
                base = base_ref[page]
                inside = jnp.logical_and(index >= base, index < base + meta_ref[page, 1])
                return jnp.where(inside, index - base + meta_ref[page, 0], key_pos)

            key_pos = lax.fori_loop(0, pages, mark, jnp.full((1, chunk), FAR, jnp.int32))
            row = tile_index * tile + lax.broadcasted_iota(jnp.int32, (tile, 1), 0)
            token = row // chip_rows * (2 * tokens_here) + lax.rem(row, chip_rows // 2) // half_heads
            s = jnp.where(key_pos <= first + token, s, NEG)
        scores[buffer, position] = s
        peak = peaks[...]
        for group in range(chunk // 128):
            peak = jnp.maximum(peak, s[:, group * 128 : (group + 1) * 128])
        peaks[...] = peak

    def mix(buffer, position):
        top = tops[buffer]
        weights = []
        for group in range(chunk // 128):
            s = scores[buffer, position, :, group * 128 : (group + 1) * 128]
            weights.append(jnp.exp2((s - top) * LOG2E_SCALE).astype(BF16))
        values = vc[pl.ds(pl.multiple_of(position * chunk, chunk), chunk), :]
        sums[...] += jnp.dot(jnp.concatenate(weights, axis=1), values, preferred_element_type=F32)

    def settle(buffer):
        tops[buffer] = jnp.broadcast_to(jnp.max(peaks[...], axis=1, keepdims=True), (tile, 128))
        peaks[...] = jnp.full_like(peaks, NEG)

    eye = lax.broadcasted_iota(jnp.int32, (128, 128), 0) == lax.broadcasted_iota(jnp.int32, (128, 128), 1)

    def finish(tile_index, buffer):
        for part in range(tile // 128):
            rows = pl.ds(part * 128, 128)
            top = tops[buffer, rows, :]
            found = top > 0.5 * NEG
            block = tile_index * (tile // 128) + part
            o_ref[block] = jnp.where(found, sums[rows, 0:HD], 0.0).astype(BF16)
            total = jnp.where(found, sums[rows, HD : 2 * HD], 0.0)
            scaled = jnp.where(found, top * LOG2E_SCALE, NEG)
            stat_ref[part % 2, 0, pl.ds(block // 2, 1), :] = jnp.sum(
                jnp.where(eye, scaled, 0.0), axis=0, keepdims=True
            )
            stat_ref[part % 2, 1, pl.ds(block // 2, 1), :] = jnp.sum(
                jnp.where(eye, total, 0.0), axis=0, keepdims=True
            )
        sums[...] = jnp.zeros_like(sums)

    peaks[...] = jnp.full_like(peaks, NEG)
    sums[...] = jnp.zeros_like(sums)
    loop(0, clear, lambda c: score(0, 0, c, False))
    loop(clear, chunks, lambda c: score(0, 0, c, True))
    settle(0)

    def turn(t):
        buffer = lax.rem(t, 2)

        def both(c, masked):
            score(t, buffer, c, masked)
            mix(1 - buffer, c)

        loop(0, clear, lambda c: both(c, False))
        loop(clear, chunks, lambda c: both(c, True))
        finish(t - 1, 1 - buffer)
        settle(buffer)

    loop(1, tiles, turn)
    final = (tiles - 1) % 2
    loop(0, chunks, lambda c: mix(final, c))
    finish(tiles - 1, final)


def attend(queries, keys, values, meta, start, tokens_here, half_heads, tile, chunk):
    rows = queries.shape[0]
    pages = meta.shape[0]
    blocks = rows // 128
    slots = pages * PAGE
    vmem = pl.BlockSpec(memory_space=pltpu.VMEM)
    smem = pl.BlockSpec(memory_space=pltpu.SMEM)
    return pl.pallas_call(
        functools.partial(attend_kernel, tile, chunk, tokens_here, half_heads),
        out_shape=(
            jax.ShapeDtypeStruct((blocks, 128, HD), BF16),
            jax.ShapeDtypeStruct((2, 2, blocks // 2, 128), F32),
        ),
        in_specs=[smem, smem, vmem, vmem, vmem],
        out_specs=(vmem, vmem),
        scratch_shapes=[
            pltpu.VMEM((slots + chunk, HD), BF16),
            pltpu.VMEM((slots + chunk, 2 * HD), BF16),
            pltpu.VMEM((2, slots // chunk, tile, chunk), F32),
            pltpu.VMEM((tile, 128), F32),
            pltpu.VMEM((2, tile, 128), F32),
            pltpu.VMEM((tile, 2 * HD), F32),
            pltpu.VMEM((16, HD), BF16),
            pltpu.SMEM((pages,), jnp.int32),
        ],
        compiler_params=pltpu.CompilerParams(vmem_limit_bytes=VMEM_LIMIT),
        name="attend",
    )(meta, start, queries, keys, values)


def split3(row):
    high = row.astype(BF16).astype(F32)
    rest = row - high
    middle = rest.astype(BF16).astype(F32)
    return high, middle, rest - middle


def finish_kernel(
    chips, layers, tokens_here, half_heads,
    o_ref, stat_ref, w_ref, att_ref, proj_ref,
    o_own, o_sib, st_own, st_sib, w, out_msg, in_msg, own_chunk, spread_out, natural, terms, z_in,
    local_sems, pair_send, pair_recv, a_send, a_recv, g_send, g_recv, s_send, s_recv, z_send, z_recv,
):
    ctx = lax.axis_index("ctx")
    layer = lax.axis_index("kvh")
    chip, core = ctx // 2, lax.rem(ctx, 2)
    other = {"ctx": chip * 2 + 1 - core}
    two = 2 * tokens_here

    load_w = pltpu.make_async_copy(w_ref, w, local_sems.at[0])
    load_o = pltpu.make_async_copy(o_ref.at[:, core], o_own, local_sems.at[1])
    load_st = pltpu.make_async_copy(stat_ref.at[core], st_own, local_sems.at[2])
    load_st.start()
    load_o.start()
    load_w.start()
    greet(
        [
            (0, 1, lambda k: other),
            (1, chips - 1, lambda k: {"ctx": lax.rem(chip + k, chips) * 2 + core}),
            (1, layers - 1, lambda k: {"kvh": lax.rem(layer + k, layers)}),
        ]
    )
    pair_st = remote(stat_ref.at[1 - core], st_sib, pair_send.at[0], pair_recv.at[0], other)
    pair_st.start()
    groups = 4 if chips % 4 == 0 else 1
    size = chips // groups
    pair_o = []
    for group in range(groups):
        here = pl.ds(group * size, size)
        copy = remote(
            o_ref.at[here, 1 - core], o_sib.at[here], pair_send.at[1 + group], pair_recv.at[1 + group], other
        )
        copy.start()
        pair_o.append(copy)
    load_st.wait()
    load_o.wait()
    pair_st.wait_recv()
    top_a, top_b = st_own[0], st_sib[0]
    top = jnp.maximum(top_a, top_b)
    scale_a, scale_b = jnp.exp2(top_a - top), jnp.exp2(top_b - top)
    total = scale_a * st_own[1] + scale_b * st_sib[1]
    pad = jnp.zeros((128 - chips, 128), F32)
    turned_a = jnp.concatenate([scale_a, pad], axis=0).T
    turned_b = jnp.concatenate([scale_b, pad], axis=0).T
    tops3, totals3 = split3(top), split3(total)
    sub = lax.broadcasted_iota(jnp.int32, (16, 128), 0)

    def message(peer):
        return remote(
            out_msg.at[peer], in_msg.at[chip], a_send.at[peer], a_recv.at[chip], {"ctx": peer * 2 + core}
        )

    for block in range(chips):
        if block % size == 0:
            pair_o[block // size].wait_recv()
        mixed = turned_a[:, block : block + 1] * o_own[block].astype(F32) + turned_b[
            :, block : block + 1
        ] * o_sib[block].astype(F32)
        out_msg[block, 0:128, :] = mixed.astype(BF16)
        lines = jnp.zeros((16, 128), F32)
        for line, value in enumerate(tops3 + totals3):
            lines = jnp.where(sub == line, jnp.broadcast_to(value[block : block + 1], (16, 128)), lines)
        out_msg[block, 128:144, :] = lines.astype(BF16)

        @pl.when(chip != block)
        def _(block=block):
            message(block).start()

    in_msg[chip] = out_msg[chip]

    def arrived(k):
        source = lax.rem(chip + k, chips)
        remote(
            out_msg.at[source], in_msg.at[source], a_send.at[source], a_recv.at[source], {"ctx": source * 2 + core}
        ).wait_recv()

    loop(1, chips, arrived)
    tops_in, totals_in = [], []
    for source in range(chips):
        lines = in_msg[source, 128:144, :].astype(F32)
        tops_in.append(lines[0:1] + lines[1:2] + lines[2:3])
        totals_in.append(lines[3:4] + lines[4:5] + lines[5:6])
    top = jnp.concatenate(tops_in, axis=0)
    scale = jnp.exp2(top - jnp.max(top, axis=0, keepdims=True))
    total = jnp.sum(scale * jnp.concatenate(totals_in, axis=0), axis=0, keepdims=True)
    turned = jnp.concatenate([scale / total, pad], axis=0).T
    attention = jnp.zeros((128, HD), F32)
    for source in range(chips):
        attention = attention + turned[:, source : source + 1] * in_msg[source, 0:128, :].astype(F32)
    row = lax.broadcasted_iota(jnp.int32, (128, 128), 0)
    column = lax.broadcasted_iota(jnp.int32, (128, 128), 1)
    swap = jnp.where(column == lax.rem(row, two) * half_heads + row // two, 1.0, 0.0).astype(BF16)
    swapped = jnp.dot(swap, attention.astype(BF16), preferred_element_type=F32).astype(BF16)
    for head in range(half_heads):
        own_chunk[:, head * HD : (head + 1) * HD] = swapped[head * two : (head + 1) * two, :]
    spread_out[chip, core] = own_chunk[...]

    def at(p, c):
        return spread_out.at[p, c]

    spread(chips, chip, core, at, own_chunk, g_send, g_recv, s_send, s_recv)
    load_w.wait()
    spread_finish(chips, chip, core, at, own_chunk, g_send, g_recv, s_send, s_recv)

    depth = half_heads * HD
    tokens = chips * two
    width = w.shape[1]
    for part in range(2):
        lhs = spread_out[:, part].reshape(tokens, depth)
        product = jnp.dot(lhs, w[part * depth : (part + 1) * depth, :], preferred_element_type=F32)
        if part == 0:
            held = product
        else:
            terms[...] = (held + product).astype(BF16).reshape(layers, tokens // layers, width)

    def deliver(k):
        peer = lax.rem(layer + k, layers)
        return remote(terms.at[peer], z_in.at[layer], z_send.at[k], z_recv.at[layer], {"kvh": peer})

    loop(1, layers, lambda k: deliver(k).start())
    z_in[layer] = terms[layer]

    for part in range(2):
        both = spread_out[chip, part].astype(F32)
        mine = jnp.where(core == 0, both[0:tokens_here], both[tokens_here:two])
        for head in range(half_heads):
            natural[pl.ds(part * half_heads + head, tokens_here, stride=2 * half_heads), :] = mine[
                :, head * HD : (head + 1) * HD
            ]
    att_ref[...] = natural[...].astype(BF16).reshape(att_ref.shape)

    def landed(k):
        source = lax.rem(layer + k, layers)
        remote(terms.at[source], z_in.at[source], z_send.at[k], z_recv.at[source], {"kvh": source}).wait_recv()

    loop(1, layers, landed)
    projected = z_in[0].astype(F32)
    for source in range(1, layers):
        projected = projected + z_in[source].astype(F32)
    proj_ref[...] = projected.astype(BF16)

    pair_st.wait_send()
    for copy in pair_o:
        copy.wait_send()
    loop(1, chips, lambda k: message(lax.rem(chip + k, chips)).wait_send())
    loop(1, layers, lambda k: deliver(k).wait_send())


def finish(mesh, partials, stats, out_weight, tokens_here, half_heads):
    chips, layers = mesh.shape["ctx"] // 2, mesh.shape["kvh"]
    two = 2 * tokens_here
    depth, width = half_heads * HD, out_weight.shape[1]
    tokens = chips * two
    groups = 4 if chips % 4 == 0 else 1
    dma = pltpu.SemaphoreType.DMA
    vmem = pl.BlockSpec(memory_space=pltpu.VMEM)
    anywhere = pl.BlockSpec(memory_space=pl.ANY)
    return pl.pallas_call(
        functools.partial(finish_kernel, chips, layers, tokens_here, half_heads),
        out_shape=(
            jax.ShapeDtypeStruct((tokens_here, 2 * half_heads, HD), BF16),
            jax.ShapeDtypeStruct((tokens // layers, width), BF16),
        ),
        in_specs=[anywhere] * 3,
        out_specs=(vmem, vmem),
        scratch_shapes=[
            pltpu.VMEM((chips, 128, HD), BF16),
            pltpu.VMEM((chips, 128, HD), BF16),
            pltpu.VMEM((2, chips, 128), F32),
            pltpu.VMEM((2, chips, 128), F32),
            pltpu.VMEM(out_weight.shape, BF16),
            pltpu.VMEM((chips, 144, HD), BF16),
            pltpu.VMEM((chips, 144, HD), BF16),
            pltpu.VMEM((two, depth), BF16),
            pltpu.VMEM((chips, 2, two, depth), BF16),
            pltpu.VMEM((2 * half_heads * tokens_here, HD), F32),
            pltpu.VMEM((layers, tokens // layers, width), BF16),
            pltpu.VMEM((layers, tokens // layers, width), BF16),
            dma((3,)),
            dma((1 + groups,)),
            dma((1 + groups,)),
            dma((chips,)),
            dma((chips,)),
            dma((chips,)),
            dma((chips,)),
            dma((chips,)),
            dma((chips,)),
            dma((layers,)),
            dma((layers,)),
        ],
        compiler_params=pltpu.CompilerParams(
            collective_id=1, has_side_effects=True, vmem_limit_bytes=VMEM_LIMIT
        ),
        name="finish",
    )(partials, stats, out_weight)


def solution(mesh, tile=512, chunk=512):
    def local(queries, key_cache, value_cache, block_lengths, block_home, stretch_start, out_weight):
        slots = key_cache.shape[0]
        pages = slots // PAGE
        tokens_here, heads, _ = queries.shape
        half_heads = heads // 2
        chips = mesh.shape["ctx"] // 2
        qall, meta = gather_queries(mesh, queries, block_lengths, block_home, pages)
        partials, stats = attend(
            qall.reshape(-1, HD),
            key_cache.reshape(slots, HD),
            value_cache.reshape(slots, HD),
            meta,
            stretch_start,
            tokens_here,
            half_heads,
            tile,
            chunk,
        )
        return finish(mesh, partials.reshape(chips, 2, 128, HD), stats, out_weight, tokens_here, half_heads)

    in_specs = (
        P("ctx", "kvh", None),
        P("ctx", "kvh", None),
        P("ctx", "kvh", None),
        P(),
        P(),
        P(),
        P("kvh", "ctx"),
    )
    out_specs = (P("ctx", "kvh", None), P("kvh", "ctx"))
    return jax.shard_map(local, mesh=mesh, in_specs=in_specs, out_specs=out_specs, check_vma=False)
```

```python
import functools
import math

import jax
import jax.numpy as jnp
from jax import lax
from jax.experimental import pallas as pl
from jax.experimental.pallas import tpu as pltpu
from jax.sharding import PartitionSpec as P

HD = 128
PAGE = 256
HEADS_HERE = 16
NEG = -1e30
FAR = 1 << 30
LOG2E_SCALE = math.log2(math.e) / math.sqrt(HD)
F32 = jnp.float32
BF16 = jnp.bfloat16
VMEM_LIMIT = 56 * 1024 * 1024


def greet(devices):
    barrier = pltpu.get_barrier_semaphore()
    count = 0
    for first, number, device_of in devices:
        count += number

        def body(k, _, device_of=device_of):
            pl.semaphore_signal(
                barrier, inc=1, device_id=device_of(k), device_id_type=pl.DeviceIdType.MESH
            )
            return 0

        lax.fori_loop(first, first + number, body, 0)
    pl.semaphore_wait(barrier, count)


def remote(src, dst, send, recv, device):
    return pltpu.make_async_remote_copy(
        src_ref=src,
        dst_ref=dst,
        send_sem=send,
        recv_sem=recv,
        device_id=device,
        device_id_type=pl.DeviceIdType.MESH,
    )


def loop(start, stop, body):
    def step(k, _):
        body(k)
        return 0

    lax.fori_loop(start, stop, step, 0)


def spread(chips, chip, core, at, own, send, recv, sib_send, sib_recv):
    other = {"ctx": chip * 2 + 1 - core}

    def start(k):
        peer = lax.rem(chip + k, chips)
        remote(own, at(chip, core), send.at[k], recv.at[chip], {"ctx": peer * 2 + core}).start()

    loop(1, chips, start)
    remote(own, at(chip, core), sib_send.at[chip], sib_recv.at[chip], other).start()

    def forward(k):
        source = lax.rem(chip + k, chips)
        here = at(source, core)
        remote(own, here, send.at[k], recv.at[source], {"ctx": source * 2 + core}).wait_recv()
        remote(here, here, sib_send.at[source], sib_recv.at[source], other).start()

    loop(1, chips, forward)


def spread_arrived(chips, chip, core, at, own, sib_send, sib_recv):
    other = {"ctx": chip * 2 + 1 - core}

    def finish(source):
        there = at(source, 1 - core)
        remote(own, there, sib_send.at[source], sib_recv.at[source], other).wait_recv()

    loop(0, chips, finish)


def spread_sent(chips, chip, core, at, own, send, recv, sib_send, sib_recv):
    other = {"ctx": chip * 2 + 1 - core}

    def sent(k):
        peer = lax.rem(chip + k, chips)
        remote(own, at(chip, core), send.at[k], recv.at[chip], {"ctx": peer * 2 + core}).wait_send()

    loop(1, chips, sent)

    def passed(source):
        here = at(source, core)
        remote(here, here, sib_send.at[source], sib_recv.at[source], other).wait_send()

    loop(0, chips, passed)


def gather_kernel(
    devices, q_ref, len_ref, home_ref, k_ref, v_ref, qall_ref, k_out, v_out, meta_ref,
    mine, natural, send, recv, kv_send, kv_recv, own_sem,
):
    ctx = lax.axis_index("ctx")
    core = lax.rem(ctx, 2)
    other = {"ctx": ctx + 1 - 2 * core}
    tokens, heads = q_ref.shape[0], q_ref.shape[1]
    half = heads // 2
    natural[...] = q_ref[...].astype(F32).reshape(tokens * heads, HD)
    for part in range(2):
        rows = [natural[pl.ds(part * half + head, tokens, stride=heads), :] for head in range(half)]
        mine[part] = jnp.concatenate(rows, axis=0).astype(BF16)
    greet([(1, devices - 1, lambda k: {"ctx": lax.rem(ctx + k, devices)})])

    def send_to(k):
        peer = lax.rem(ctx + k, devices)
        return remote(mine.at[lax.rem(peer, 2)], qall_ref.at[ctx], send.at[k], recv.at[ctx], {"ctx": peer})

    loop(1, devices, lambda k: send_to(k).start())
    own = pltpu.make_async_copy(mine.at[core], qall_ref.at[ctx], own_sem)
    own.start()
    pairs = [
        remote(k_ref, k_out, kv_send.at[0], kv_recv.at[0], other),
        remote(v_ref, v_out, kv_send.at[1], kv_recv.at[1], other),
    ]
    for pair in pairs:
        pair.start()

    pages, blocks = meta_ref.shape[0], home_ref.shape[1]
    lengths = len_ref[...].astype(F32)
    index = lax.broadcasted_iota(jnp.int32, (pages, blocks), 0)
    here = pages // 2
    stored = jnp.where(index < here, ctx * here + index, (ctx + 1 - 2 * core) * here + index - here)
    logical = lax.broadcasted_iota(jnp.int32, (pages, blocks), 1).astype(F32)
    match = home_ref[...] == stored
    place = jnp.sum(jnp.where(match, logical, 0.0), axis=1, keepdims=True)
    filled = jnp.sum(jnp.where(match, lengths, 0.0), axis=1, keepdims=True)
    begin = jnp.sum(jnp.where(logical < place, lengths, 0.0), axis=1, keepdims=True)
    lane = lax.broadcasted_iota(jnp.int32, (pages, 128), 1)
    meta = jnp.where(lane == 0, begin, jnp.where(lane == 1, filled, 0.0))
    meta_ref[...] = meta.astype(jnp.int32)

    own.wait()

    def arrived(k):
        source = lax.rem(ctx + k, devices)
        remote(mine.at[0], qall_ref.at[source], send.at[k], recv.at[source], {"ctx": source}).wait_recv()

    loop(1, devices, arrived)
    for pair in pairs:
        pair.wait()
    loop(1, devices, lambda k: send_to(k).wait_send())


def gather_queries(mesh, queries, block_lengths, block_home, keys, values):
    devices = mesh.shape["ctx"]
    tokens, heads, _ = queries.shape
    rows = tokens * heads // 2
    pages = 2 * keys.shape[0] // PAGE
    dma = pltpu.SemaphoreType.DMA
    vmem = pl.BlockSpec(memory_space=pltpu.VMEM)
    anywhere = pl.BlockSpec(memory_space=pl.ANY)
    return pl.pallas_call(
        functools.partial(gather_kernel, devices),
        out_shape=(
            jax.ShapeDtypeStruct((devices, rows, HD), BF16),
            jax.ShapeDtypeStruct(keys.shape, BF16),
            jax.ShapeDtypeStruct(values.shape, BF16),
            jax.ShapeDtypeStruct((pages, 128), jnp.int32),
        ),
        in_specs=[vmem] * 3 + [anywhere] * 2,
        out_specs=(anywhere, anywhere, anywhere, vmem),
        scratch_shapes=[
            pltpu.VMEM((2, rows, HD), BF16),
            pltpu.VMEM((2 * rows, HD), F32),
            dma((devices,)),
            dma((devices,)),
            dma((2,)),
            dma((2,)),
            dma,
        ],
        compiler_params=pltpu.CompilerParams(collective_id=0, has_side_effects=True),
        name="gather_queries",
    )(queries, block_lengths.reshape(1, -1), block_home.reshape(1, -1), keys, values)


def attend_kernel(
    tile, chunk,
    meta_ref, start_ref, q_ref, k_a, v_a, k_b, v_b, msg_ref,
    k_in, v_in, k_sem, v_sem, kc, vc, qh, bias, scores_a, scores_b, peaks, tops_a, tops_b, sums, tail, base_ref,
):
    pages = meta_ref.shape[0]
    heads, tokens, _ = qh.shape
    devices = q_ref.shape[0]
    tokens_here = tokens // devices
    tiles = heads * tokens // tile
    first = start_ref[0]
    last = first + tokens - 1
    slot = lax.broadcasted_iota(jnp.int32, (PAGE, HD), 0)

    here = pages // 2

    def fetch(page, keys, values):
        source = pl.ds(pl.multiple_of(lax.rem(page, here) * PAGE, PAGE), PAGE)
        return (
            pltpu.make_async_copy(keys.at[source, :], k_in.at[page], k_sem.at[page]),
            pltpu.make_async_copy(values.at[source, :], v_in.at[page], v_sem.at[page]),
        )

    def request(page, keys, values):
        @pl.when(meta_ref[page, 0] <= last)
        def _():
            for copy in fetch(page, keys, values):
                copy.start()

    loop(0, here, lambda p: request(p, k_a, v_a))
    loop(here, pages, lambda p: request(p, k_b, v_b))

    def arrange(chip):
        block = q_ref[pl.ds(2 * chip, 2)].astype(F32).reshape(2, heads, tokens_here, HD)
        for head in range(heads):
            rows = jnp.concatenate([block[0, head], block[1, head]], axis=0)
            target = pl.ds(pl.multiple_of(chip * 2 * tokens_here, 2 * tokens_here), 2 * tokens_here)
            qh[head, target, :] = rows.astype(BF16)

    loop(0, devices // 2, arrange)

    def visit(page, used, masked):
        begin, filled = meta_ref[page, 0], meta_ref[page, 1]
        partly = begin + filled - 1 > first
        seen = begin <= last
        take = jnp.logical_and(seen, partly) if masked else jnp.logical_not(partly)

        @pl.when(take)
        def _():
            base_ref[page] = used
            target = pl.ds(pl.multiple_of(used, 16), PAGE)
            for copy in fetch(page, k_a, v_a):
                copy.wait()
            keys = k_in[page].astype(F32)
            live = slot < filled
            lead = jnp.broadcast_to(keys[0:1, :], (PAGE, HD))
            kc[target, :] = jnp.where(live, keys, lead).astype(BF16)
            tail[...] = lead[0:16, :].astype(BF16)
            values = v_in[page].astype(F32)
            vc[target, 0:HD] = jnp.where(live, values, 0.0).astype(BF16)
            vc[target, HD : 2 * HD] = jnp.where(live, 1.0, 0.0).astype(BF16)

        if not masked:

            @pl.when(jnp.logical_not(take))
            def _():
                base_ref[page] = FAR

        return used + jnp.where(take, (filled + 15) // 16 * 16, 0)

    tail[...] = jnp.zeros_like(tail)
    plain = lax.fori_loop(0, pages, lambda p, u: visit(p, u, False), jnp.int32(0))
    used = lax.fori_loop(0, pages, lambda p, u: visit(p, u, True), plain)
    for piece in range(chunk // 16):
        target = pl.ds(pl.multiple_of(used + piece * 16, 16), 16)
        kc[target, :] = tail[...]
        vc[target, :] = jnp.zeros((16, 2 * HD), BF16)
    chunks = (used + chunk - 1) // chunk
    clear = jnp.where(used > plain, plain // chunk, chunks)
    per_tile = tile // tokens

    def shade(position):
        index = position * chunk + lax.broadcasted_iota(jnp.int32, (1, chunk), 1)

        def mark(page, key_pos):
            base = base_ref[page]
            inside = jnp.logical_and(index >= base, index < base + meta_ref[page, 1])
            return jnp.where(inside, index - base + meta_ref[page, 0], key_pos)

        key_pos = lax.fori_loop(0, pages, mark, jnp.full((1, chunk), FAR, jnp.int32))
        token = lax.broadcasted_iota(jnp.int32, (tokens, 1), 0)
        bias[position] = jnp.where(key_pos <= first + token, 0.0, NEG).astype(BF16)

    loop(clear, chunks, shade)

    def score(tile_index, scores, position, masked, part):
        q = qh[tile_index * per_tile + part]
        keys = kc[pl.ds(pl.multiple_of(position * chunk, chunk), chunk), :]
        s = lax.dot_general(q, keys, (((1,), (1,)), ((), ())), preferred_element_type=F32)
        if masked:
            s = s + bias[position].astype(F32)
        rows = pl.ds(part * tokens, tokens)
        scores[position, rows, :] = s
        peak = peaks[rows, :]
        for group in range(chunk // 128):
            peak = jnp.maximum(peak, s[:, group * 128 : (group + 1) * 128])
        peaks[rows, :] = peak

    def mix(scores, tops, position, part):
        rows = pl.ds(part * tokens, tokens)
        top = tops[rows, :]
        weights = []
        for group in range(chunk // 128):
            s = scores[position, rows, group * 128 : (group + 1) * 128]
            weights.append(jnp.exp2((s - top) * LOG2E_SCALE).astype(BF16))
        values = vc[pl.ds(pl.multiple_of(position * chunk, chunk), chunk), :]
        sums[rows, :] += jnp.dot(jnp.concatenate(weights, axis=1), values, preferred_element_type=F32)

    def settle(tops):
        tops[...] = jnp.broadcast_to(jnp.max(peaks[...], axis=1, keepdims=True), (tile, 128))
        peaks[...] = jnp.full_like(peaks, NEG)

    eye = lax.broadcasted_iota(jnp.int32, (128, 128), 0) == lax.broadcasted_iota(jnp.int32, (128, 128), 1)
    sub = lax.broadcasted_iota(jnp.int32, (16, 128), 0)

    def finish(tile_index, tops):
        for part in range(tile // 128):
            rows = pl.ds(part * 128, 128)
            top = tops[rows, :]
            found = top > 0.5 * NEG
            block = tile_index * (tile // 128) + part
            msg_ref[block, 0:128, :] = jnp.where(found, sums[rows, 0:HD], 0.0).astype(BF16)
            total = jnp.where(found, sums[rows, HD : 2 * HD], 0.0)
            scaled = jnp.where(found, top * LOG2E_SCALE, NEG)
            tops_row = jnp.sum(jnp.where(eye, scaled, 0.0), axis=0, keepdims=True)
            totals_row = jnp.sum(jnp.where(eye, total, 0.0), axis=0, keepdims=True)
            lines = jnp.zeros((16, 128), F32)
            for line, value in enumerate(split3(tops_row) + split3(totals_row)):
                lines = jnp.where(sub == line, jnp.broadcast_to(value, (16, 128)), lines)
            msg_ref[block, 128:144, :] = lines.astype(BF16)
        sums[...] = jnp.zeros_like(sums)

    peaks[...] = jnp.full_like(peaks, NEG)
    sums[...] = jnp.zeros_like(sums)

    def score_all(c, masked):
        for part in range(per_tile):
            score(0, scores_a, c, masked, part)

    loop(0, clear, lambda c: score_all(c, False))
    loop(clear, chunks, lambda c: score_all(c, True))
    settle(tops_a)

    def turn(t, scores, tops, scores_before, tops_before):
        def both(c, masked):
            for part in range(per_tile):
                score(t, scores, c, masked, part)
                mix(scores_before, tops_before, c, part)

        loop(0, clear, lambda c: both(c, False))
        loop(clear, chunks, lambda c: both(c, True))
        finish(t - 1, tops_before)
        settle(tops)

    def pair(u):
        turn(2 * u + 1, scores_b, tops_b, scores_a, tops_a)

        @pl.when(2 * u + 2 < tiles)
        def _():
            turn(2 * u + 2, scores_a, tops_a, scores_b, tops_b)

    loop(0, tiles // 2, pair)

    def mix_all(c):
        for part in range(per_tile):
            mix(scores_b, tops_b, c, part)

    loop(0, chunks, mix_all)
    finish(tiles - 1, tops_b)


def attend(queries, keys, values, keys_b, values_b, meta, start, tile, chunk):
    devices, rows, _ = queries.shape
    pages = meta.shape[0]
    slots = pages * PAGE
    heads = HEADS_HERE // 2
    tokens = devices * rows // heads
    dma = pltpu.SemaphoreType.DMA
    vmem = pl.BlockSpec(memory_space=pltpu.VMEM)
    smem = pl.BlockSpec(memory_space=pltpu.SMEM)
    anywhere = pl.BlockSpec(memory_space=pl.ANY)
    return pl.pallas_call(
        functools.partial(attend_kernel, tile, chunk),
        out_shape=jax.ShapeDtypeStruct((heads * tokens // 128, 144, HD), BF16),
        in_specs=[smem, smem, vmem] + [anywhere] * 4,
        out_specs=vmem,
        scratch_shapes=[
            pltpu.VMEM((pages, PAGE, HD), BF16),
            pltpu.VMEM((pages, PAGE, HD), BF16),
            dma((pages,)),
            dma((pages,)),
            pltpu.VMEM((slots + chunk, HD), BF16),
            pltpu.VMEM((slots + chunk, 2 * HD), BF16),
            pltpu.VMEM((heads, tokens, HD), BF16),
            pltpu.VMEM((slots // chunk, tokens, chunk), BF16),
            pltpu.VMEM((slots // chunk, tile, chunk), F32),
            pltpu.VMEM((slots // chunk, tile, chunk), F32),
            pltpu.VMEM((tile, 128), F32),
            pltpu.VMEM((tile, 128), F32),
            pltpu.VMEM((tile, 128), F32),
            pltpu.VMEM((tile, 2 * HD), F32),
            pltpu.VMEM((16, HD), BF16),
            pltpu.SMEM((pages,), jnp.int32),
        ],
        compiler_params=pltpu.CompilerParams(vmem_limit_bytes=VMEM_LIMIT),
        name="attend",
    )(meta, start, queries, keys, values, keys_b, values_b)


def split3(row):
    high = row.astype(BF16).astype(F32)
    rest = row - high
    middle = rest.astype(BF16).astype(F32)
    return high, middle, rest - middle


def finish_kernel(
    chips, layers, msg_ref, w_ref, att_ref, proj_ref,
    w, in_msg, own_chunk, gathered, natural, terms, z_in,
    local_sems, a_send, a_recv, g_send, g_recv, s_send, s_recv, z_send, z_recv,
):
    ctx = lax.axis_index("ctx")
    layer = lax.axis_index("kvh")
    chip, core = ctx // 2, lax.rem(ctx, 2)
    tokens_here, heads, _ = att_ref.shape
    load_w = pltpu.make_async_copy(w_ref, w, local_sems.at[0])
    load_own = pltpu.make_async_copy(msg_ref.at[chip], in_msg.at[chip], local_sems.at[1])
    load_own.start()
    load_w.start()
    greet(
        [
            (0, 1, lambda k: {"ctx": ctx + 1 - 2 * core}),
            (1, chips - 1, lambda k: {"ctx": lax.rem(chip + k, chips) * 2 + core}),
            (1, layers - 1, lambda k: {"kvh": lax.rem(layer + k, layers)}),
        ]
    )

    def message(k):
        peer = lax.rem(chip + k, chips)
        return remote(msg_ref.at[peer], in_msg.at[chip], a_send.at[k], a_recv.at[chip], {"ctx": peer * 2 + core})

    loop(1, chips, lambda k: message(k).start())

    def arrived(k):
        source = lax.rem(chip + k, chips)
        remote(
            msg_ref.at[source], in_msg.at[source], a_send.at[k], a_recv.at[source], {"ctx": source * 2 + core}
        ).wait_recv()

    load_own.wait()
    loop(1, chips, arrived)
    tops_in, totals_in = [], []
    for source in range(chips):
        lines = in_msg[source, 128:144, :].astype(F32)
        tops_in.append(lines[0:1] + lines[1:2] + lines[2:3])
        totals_in.append(lines[3:4] + lines[4:5] + lines[5:6])
    top = jnp.concatenate(tops_in, axis=0)
    scale = jnp.exp2(top - jnp.max(top, axis=0, keepdims=True))
    total = jnp.sum(scale * jnp.concatenate(totals_in, axis=0), axis=0, keepdims=True)
    pad = jnp.zeros((128 - chips, 128), F32)
    turned = jnp.concatenate([scale / total, pad], axis=0).T
    attention = jnp.zeros((128, HD), F32)
    for source in range(chips):
        attention = attention + turned[:, source : source + 1] * in_msg[source, 0:128, :].astype(F32)
    own_chunk[...] = attention.astype(BF16)
    gathered[core, chip] = own_chunk[...]

    def at(p, c):
        return gathered.at[c, p]

    spread(chips, chip, core, at, own_chunk, g_send, g_recv, s_send, s_recv)
    load_w.wait()

    parts = gathered.shape[1]
    half_heads = heads // 2
    split = parts // half_heads
    tokens, depth = split * 128, half_heads * HD
    width = w.shape[1]

    def product(which):
        columns = [
            gathered[which, head * split : (head + 1) * split].reshape(tokens, HD) for head in range(half_heads)
        ]
        rows = pl.ds(pl.multiple_of(which * depth, depth), depth)
        return jnp.dot(jnp.concatenate(columns, axis=1), w[rows, :], preferred_element_type=F32)

    held = product(core)
    spread_arrived(chips, chip, core, at, own_chunk, s_send, s_recv)
    terms[...] = (held + product(1 - core)).astype(BF16).reshape(layers, tokens // layers, width)

    def deliver(k):
        peer = lax.rem(layer + k, layers)
        return remote(terms.at[peer], z_in.at[layer], z_send.at[k], z_recv.at[layer], {"kvh": peer})

    loop(1, layers, lambda k: deliver(k).start())
    z_in[layer] = terms[layer]

    two = 2 * tokens_here
    per_part = 128 // two
    line = pl.ds(pl.multiple_of(lax.rem(chip, per_part) * two, two), two)
    for head in range(heads):
        both = gathered[head // half_heads, lax.rem(head, half_heads) * split + chip // per_part, line, :].astype(F32)
        mine = jnp.where(core == 0, both[0:tokens_here], both[tokens_here:two])
        natural[pl.ds(head, tokens_here, stride=heads), :] = mine
    att_ref[...] = natural[...].astype(BF16).reshape(att_ref.shape)

    def landed(k):
        source = lax.rem(layer + k, layers)
        remote(terms.at[source], z_in.at[source], z_send.at[k], z_recv.at[source], {"kvh": source}).wait_recv()

    loop(1, layers, landed)
    projected = z_in[0].astype(F32)
    for source in range(1, layers):
        projected = projected + z_in[source].astype(F32)
    proj_ref[...] = projected.astype(BF16)

    loop(1, chips, lambda k: message(k).wait_send())
    spread_sent(chips, chip, core, at, own_chunk, g_send, g_recv, s_send, s_recv)
    loop(1, layers, lambda k: deliver(k).wait_send())


def finish(mesh, messages, out_weight, tokens_here):
    chips, layers = mesh.shape["ctx"] // 2, mesh.shape["kvh"]
    width = out_weight.shape[1]
    tokens = chips * 2 * tokens_here
    dma = pltpu.SemaphoreType.DMA
    vmem = pl.BlockSpec(memory_space=pltpu.VMEM)
    anywhere = pl.BlockSpec(memory_space=pl.ANY)
    parts = messages.shape[0]
    return pl.pallas_call(
        functools.partial(finish_kernel, chips, layers),
        out_shape=(
            jax.ShapeDtypeStruct((tokens_here, HEADS_HERE, HD), BF16),
            jax.ShapeDtypeStruct((tokens // layers, width), BF16),
        ),
        in_specs=[anywhere] * 2,
        out_specs=(vmem, vmem),
        scratch_shapes=[
            pltpu.VMEM(out_weight.shape, BF16),
            pltpu.VMEM((chips, 144, HD), BF16),
            pltpu.VMEM((128, HD), BF16),
            pltpu.VMEM((2, parts, 128, HD), BF16),
            pltpu.VMEM((HEADS_HERE * tokens_here, HD), F32),
            pltpu.VMEM((layers, tokens // layers, width), BF16),
            pltpu.VMEM((layers, tokens // layers, width), BF16),
            dma((2,)),
            dma((chips,)),
            dma((chips,)),
            dma((chips,)),
            dma((chips,)),
            dma((chips,)),
            dma((chips,)),
            dma((layers,)),
            dma((layers,)),
        ],
        compiler_params=pltpu.CompilerParams(
            collective_id=1, has_side_effects=True, vmem_limit_bytes=VMEM_LIMIT
        ),
        name="finish",
    )(messages, out_weight)


def solution(mesh, tile=512, chunk=512):
    def local(queries, key_cache, value_cache, block_lengths, block_home, stretch_start, out_weight):
        slots = key_cache.shape[0]
        keys, values = key_cache.reshape(slots, HD), value_cache.reshape(slots, HD)
        qall, keys_b, values_b, meta = gather_queries(mesh, queries, block_lengths, block_home, keys, values)
        messages = attend(qall, keys, values, keys_b, values_b, meta, stretch_start, tile, chunk)
        return finish(mesh, messages, out_weight, queries.shape[0])

    in_specs = (
        P("ctx", "kvh", None),
        P("ctx", "kvh", None),
        P("ctx", "kvh", None),
        P(),
        P(),
        P(),
        P("kvh", "ctx"),
    )
    out_specs = (P("ctx", "kvh", None), P("kvh", "ctx"))
    return jax.shard_map(local, mesh=mesh, in_specs=in_specs, out_specs=out_specs, check_vma=False)
```

```python
import functools
import math

import jax
import jax.numpy as jnp
from jax import lax
from jax.experimental import pallas as pl
from jax.experimental.pallas import tpu as pltpu
from jax.sharding import PartitionSpec as P

HD = 128
PAGE = 256
HEADS_HERE = 16
SUB = 256
NEG = -1e30
FAR = 1 << 30
LOG2E_SCALE = math.log2(math.e) / math.sqrt(HD)
F32 = jnp.float32
BF16 = jnp.bfloat16
VMEM_LIMIT = 56 * 1024 * 1024


def greet_start(devices):
    for device in devices:
        pl.semaphore_signal(
            pltpu.get_barrier_semaphore(), inc=1, device_id=device, device_id_type=pl.DeviceIdType.MESH
        )


def remote(src, dst, send, recv, device):
    return pltpu.make_async_remote_copy(
        src_ref=src,
        dst_ref=dst,
        send_sem=send,
        recv_sem=recv,
        device_id=device,
        device_id_type=pl.DeviceIdType.MESH,
    )


def loop(start, stop, body):
    def step(k, _):
        body(k)
        return 0

    lax.fori_loop(start, stop, step, 0)


def partner(chip, chips, step):
    if chips != 16:
        return lax.rem(chip + step, chips)
    return lax.rem(chip // 4 + step // 4, 4) * 4 + lax.rem(chip + step, 4)


def steps(chips):
    if chips != 16:
        return list(range(1, chips))
    near = [0, 1, 2, 1]
    return sorted(range(1, chips), key=lambda step: -(near[step // 4] + near[step % 4]))


def landed(buffer, sem):
    pltpu.make_async_copy(buffer, buffer, sem).wait()


def gather_kernel(
    devices, q_ref, len_ref, home_ref, k_ref, v_ref, qall_ref, k_out, v_out, meta_ref,
    q_in, len_in, home_in, mine, natural, send, recv, kv_send, kv_recv, own_sem, in_sems,
):
    ctx = lax.axis_index("ctx")
    core = lax.rem(ctx, 2)
    other = {"ctx": ctx + 1 - 2 * core}
    tokens, heads = q_ref.shape[0], q_ref.shape[1]
    half = heads // 2
    loads = [
        pltpu.make_async_copy(source, target, in_sems.at[i])
        for i, (source, target) in enumerate([(q_ref, q_in), (len_ref, len_in), (home_ref, home_in)])
    ]
    for load in loads:
        load.start()
    chip, chips = ctx // 2, devices // 2
    peers = [partner(chip, chips, step) * 2 + side for step in steps(chips) for side in range(2)]
    peers.append(ctx + 1 - 2 * core)
    greet_start([{"ctx": peer} for peer in peers])
    loads[0].wait()
    natural[...] = q_in[...].astype(F32).reshape(tokens * heads, HD)
    for part in range(2):
        rows = [natural[pl.ds(part * half + head, tokens, stride=heads), :] for head in range(half)]
        mine[part] = jnp.concatenate(rows, axis=0).astype(BF16)
    pl.semaphore_wait(pltpu.get_barrier_semaphore(), devices - 1)

    for peer in peers:
        remote(mine.at[lax.rem(peer, 2)], qall_ref.at[ctx], send, recv, {"ctx": peer}).start()
    own = pltpu.make_async_copy(mine.at[core], qall_ref.at[ctx], own_sem)
    own.start()
    pairs = [
        remote(k_ref, k_out, kv_send.at[0], kv_recv.at[0], other),
        remote(v_ref, v_out, kv_send.at[1], kv_recv.at[1], other),
    ]
    for pair in pairs:
        pair.start()

    pages, blocks = meta_ref.shape[0], home_ref.shape[1]
    loads[1].wait()
    loads[2].wait()
    lengths = len_in[...].astype(F32)
    index = lax.broadcasted_iota(jnp.int32, (pages, blocks), 0)
    here = pages // 2
    stored = jnp.where(index < here, ctx * here + index, (ctx + 1 - 2 * core) * here + index - here)
    logical = lax.broadcasted_iota(jnp.int32, (pages, blocks), 1).astype(F32)
    match = home_in[...] == stored
    place = jnp.sum(jnp.where(match, logical, 0.0), axis=1, keepdims=True)
    filled = jnp.sum(jnp.where(match, lengths, 0.0), axis=1, keepdims=True)
    begin = jnp.sum(jnp.where(logical < place, lengths, 0.0), axis=1, keepdims=True)
    lane = lax.broadcasted_iota(jnp.int32, (pages, 128), 1)
    meta = jnp.where(lane == 0, begin, jnp.where(lane == 1, filled, 0.0))
    meta_ref[...] = meta.astype(jnp.int32)

    own.wait()

    others = qall_ref.at[pl.ds(0, devices - 1)]
    landed(others, recv)
    for pair in pairs:
        pair.wait()
    landed(others, send)


def gather_queries(mesh, queries, block_lengths, block_home, keys, values):
    devices = mesh.shape["ctx"]
    tokens, heads, _ = queries.shape
    rows = tokens * heads // 2
    pages = 2 * keys.shape[0] // PAGE
    dma = pltpu.SemaphoreType.DMA
    vmem = pl.BlockSpec(memory_space=pltpu.VMEM)
    anywhere = pl.BlockSpec(memory_space=pl.ANY)
    return pl.pallas_call(
        functools.partial(gather_kernel, devices),
        out_shape=(
            jax.ShapeDtypeStruct((devices, rows, HD), BF16),
            jax.ShapeDtypeStruct(keys.shape, BF16),
            jax.ShapeDtypeStruct(values.shape, BF16),
            jax.ShapeDtypeStruct((pages, 128), jnp.int32),
        ),
        in_specs=[anywhere] * 5,
        out_specs=(anywhere, anywhere, anywhere, vmem),
        scratch_shapes=[
            pltpu.VMEM(queries.shape, BF16),
            pltpu.VMEM((1, block_lengths.shape[0]), jnp.int32),
            pltpu.VMEM((1, block_home.shape[0]), jnp.int32),
            pltpu.VMEM((2, rows, HD), BF16),
            pltpu.VMEM((2 * rows, HD), F32),
            dma,
            dma,
            dma((2,)),
            dma((2,)),
            dma,
            dma((3,)),
        ],
        compiler_params=pltpu.CompilerParams(
            collective_id=0, has_side_effects=True, vmem_limit_bytes=VMEM_LIMIT
        ),
        name="gather_queries",
    )(queries, block_lengths.reshape(1, -1), block_home.reshape(1, -1), keys, values)


def attend_kernel(
    chunk, layers,
    meta_ref, start_ref, q_ref, k_a, v_a, k_b, v_b, msg_ref,
    q_in, q_sem, k_in, v_in, k_sem, v_sem, kc, vc, qh, bias, scores, peaks, tops, sums, tail, base_ref,
):
    pages = meta_ref.shape[0]
    pieces, heads, piece, _ = qh.shape
    devices = q_ref.shape[0]
    tile = heads * piece
    tokens = pieces * piece
    tokens_here = tokens // devices
    two = 2 * tokens_here
    per_layer = tokens // layers
    first = start_ref[0]
    last = first + tokens - 1
    slot = lax.broadcasted_iota(jnp.int32, (PAGE, HD), 0)
    here = pages // 2

    def fetch(page, keys, values):
        source = pl.ds(pl.multiple_of(lax.rem(page, here) * PAGE, PAGE), PAGE)
        return (
            pltpu.make_async_copy(keys.at[source, :], k_in.at[page], k_sem.at[page]),
            pltpu.make_async_copy(values.at[source, :], v_in.at[page], v_sem.at[page]),
        )

    def request(page, keys, values):
        @pl.when(meta_ref[page, 0] <= last)
        def _():
            for copy in fetch(page, keys, values):
                copy.start()

    load_q = pltpu.make_async_copy(q_ref, q_in, q_sem)
    load_q.start()
    loop(0, here, lambda p: request(p, k_a, v_a))
    loop(here, pages, lambda p: request(p, k_b, v_b))

    def arrange(chip):
        block = q_in[pl.ds(2 * chip, 2)].astype(F32).reshape(2, heads, tokens_here, HD)
        layer = chip * two // per_layer
        line = layer // pieces * per_layer + lax.rem(chip * two, per_layer)
        target = pl.ds(pl.multiple_of(line, two), two)
        for head in range(heads):
            rows = jnp.concatenate([block[0, head], block[1, head]], axis=0)
            qh[lax.rem(layer, pieces), head, target, :] = rows.astype(BF16)

    def visit(page, used, masked):
        begin, filled = meta_ref[page, 0], meta_ref[page, 1]
        partly = begin + filled - 1 > first
        seen = begin <= last
        take = jnp.logical_and(seen, partly) if masked else jnp.logical_not(partly)

        @pl.when(take)
        def _():
            base_ref[page] = used
            target = pl.ds(pl.multiple_of(used, 16), PAGE)
            for copy in fetch(page, k_a, v_a):
                copy.wait()
            keys = k_in[page].astype(F32)
            live = slot < filled
            lead = jnp.broadcast_to(keys[0:1, :], (PAGE, HD))
            kc[target, :] = jnp.where(live, keys, lead).astype(BF16)
            tail[...] = lead[0:16, :].astype(BF16)
            values = v_in[page].astype(F32)
            vc[target, 0:HD] = jnp.where(live, values, 0.0).astype(BF16)
            vc[target, HD : 2 * HD] = jnp.where(live, 1.0, 0.0).astype(BF16)

        if not masked:

            @pl.when(jnp.logical_not(take))
            def _():
                base_ref[page] = FAR

        return used + jnp.where(take, (filled + 15) // 16 * 16, 0)

    tail[...] = jnp.zeros_like(tail)
    plain = lax.fori_loop(0, pages, lambda p, u: visit(p, u, False), jnp.int32(0))
    used = lax.fori_loop(0, pages, lambda p, u: visit(p, u, True), plain)
    for part in range(chunk // 16):
        target = pl.ds(pl.multiple_of(used + part * 16, 16), 16)
        kc[target, :] = tail[...]
        vc[target, :] = jnp.zeros((16, 2 * HD), BF16)
    load_q.wait()
    loop(0, devices // 2, arrange)
    chunks = (used + chunk - 1) // chunk
    clear = jnp.where(used > plain, plain // chunk, chunks)
    per_part = SUB // piece
    parts = tile // SUB

    def shade(position):
        index = position * chunk + lax.broadcasted_iota(jnp.int32, (1, chunk), 1)

        def mark(page, key_pos):
            base = base_ref[page]
            inside = jnp.logical_and(index >= base, index < base + meta_ref[page, 1])
            return jnp.where(inside, index - base + meta_ref[page, 0], key_pos)

        key_pos = lax.fori_loop(0, pages, mark, jnp.full((1, chunk), FAR, jnp.int32))
        line = lax.broadcasted_iota(jnp.int32, (piece, 1), 0)
        for s in range(pieces):
            token = (line // per_layer * pieces + s) * per_layer + lax.rem(line, per_layer)
            bias[s, position] = jnp.where(key_pos <= first + token, 0.0, NEG).astype(BF16)

    loop(clear, chunks, shade)

    def score(tile_index, position, masked, part):
        q = qh[tile_index, part * per_part : (part + 1) * per_part].reshape(SUB, HD)
        keys = kc[pl.ds(pl.multiple_of(position * chunk, chunk), chunk), :]
        s = lax.dot_general(q, keys, (((1,), (1,)), ((), ())), preferred_element_type=F32)
        if masked:
            shadow = bias[tile_index, position].astype(F32)
            s = s + jnp.concatenate([shadow] * per_part, axis=0)
        rows = pl.ds(part * SUB, SUB)
        scores[position, rows, :] = s
        peak = peaks[rows, :]
        for group in range(chunk // 128):
            peak = jnp.maximum(peak, s[:, group * 128 : (group + 1) * 128])
        peaks[rows, :] = peak

    def mix(position, part):
        rows = pl.ds(part * SUB, SUB)
        top = tops[rows, :]
        weights = []
        for group in range(chunk // 128):
            s = scores[position, rows, group * 128 : (group + 1) * 128]
            weights.append(jnp.exp2((s - top) * LOG2E_SCALE).astype(BF16))
        values = vc[pl.ds(pl.multiple_of(position * chunk, chunk), chunk), :]
        sums[rows, :] += jnp.dot(jnp.concatenate(weights, axis=1), values, preferred_element_type=F32)

    def settle():
        tops[...] = jnp.broadcast_to(jnp.max(peaks[...], axis=1, keepdims=True), (tile, 128))

    sub = lax.broadcasted_iota(jnp.int32, (16, 128), 0)
    lane = lax.broadcasted_iota(jnp.int32, (128, 128), 1)
    blocks = tile // 128

    def finish(tile_index):
        packed = jnp.zeros((128, 128), F32)
        for block in range(blocks):
            rows = pl.ds(block * 128, 128)
            packed = jnp.where(lane == block, tops[rows, :] * LOG2E_SCALE, packed)
            packed = jnp.where(lane == blocks + block, sums[rows, HD : 2 * HD], packed)
            for part in range(2):
                lines = pl.ds(block * 128 + part * 64, 64)
                msg_ref[tile_index, 2 * block + part, 0:64, :] = sums[lines, 0:HD].astype(BF16)
        stats = packed.T
        for block in range(blocks):
            lines = jnp.zeros((16, 128), F32)
            if tile_index:
                lines = msg_ref[0, 2 * block, 64:80, :].astype(F32)
            values = split3(stats[block : block + 1]) + split3(stats[blocks + block : blocks + block + 1])
            for line, value in enumerate(values):
                lines = jnp.where(sub == 6 * tile_index + line, jnp.broadcast_to(value, (16, 128)), lines)
            msg_ref[0, 2 * block, 64:80, :] = lines.astype(BF16)
            turned = jnp.concatenate([lines[:, 64:128], lines[:, 0:64]], axis=1)
            msg_ref[0, 2 * block + 1, 64:80, :] = turned.astype(BF16)

    def over_chunks(step):
        loop(0, clear, lambda c: step(c, False))
        loop(clear, chunks, lambda c: step(c, True))

    def score_all(c, masked):
        for part in range(parts):
            score(0, c, masked, part)

    peaks[...] = jnp.full_like(peaks, NEG)
    over_chunks(score_all)
    settle()

    for t in range(1, pieces):
        peaks[...] = jnp.full_like(peaks, NEG)
        sums[...] = jnp.zeros_like(sums)

        def both(c, masked, t=t):
            for part in range(parts):
                mix(c, part)
                score(t, c, masked, part)

        over_chunks(both)
        finish(t - 1)
        settle()

    def mix_all(c):
        for part in range(parts):
            mix(c, part)

    sums[...] = jnp.zeros_like(sums)
    loop(0, chunks, mix_all)
    finish(pieces - 1)


def attend(queries, keys, values, keys_b, values_b, meta, start, layers, chunk):
    devices, rows, _ = queries.shape
    pages = meta.shape[0]
    slots = pages * PAGE
    heads = HEADS_HERE // 2
    pieces = 2
    piece = devices * rows // (heads * pieces)
    tile = heads * piece
    dma = pltpu.SemaphoreType.DMA
    vmem = pl.BlockSpec(memory_space=pltpu.VMEM)
    smem = pl.BlockSpec(memory_space=pltpu.SMEM)
    anywhere = pl.BlockSpec(memory_space=pl.ANY)
    return pl.pallas_call(
        functools.partial(attend_kernel, chunk, layers),
        out_shape=jax.ShapeDtypeStruct((pieces, devices // 2, 80, HD), BF16),
        in_specs=[smem, smem] + [anywhere] * 5,
        out_specs=vmem,
        scratch_shapes=[
            pltpu.VMEM(queries.shape, BF16),
            dma,
            pltpu.VMEM((pages, PAGE, HD), BF16),
            pltpu.VMEM((pages, PAGE, HD), BF16),
            dma((pages,)),
            dma((pages,)),
            pltpu.VMEM((slots + chunk, HD), BF16),
            pltpu.VMEM((slots + chunk, 2 * HD), BF16),
            pltpu.VMEM((pieces, heads, piece, HD), BF16),
            pltpu.VMEM((pieces, slots // chunk, piece, chunk), BF16),
            pltpu.VMEM((slots // chunk, tile, chunk), F32),
            pltpu.VMEM((tile, 128), F32),
            pltpu.VMEM((tile, 128), F32),
            pltpu.VMEM((tile, 2 * HD), F32),
            pltpu.VMEM((16, HD), BF16),
            pltpu.SMEM((pages,), jnp.int32),
        ],
        compiler_params=pltpu.CompilerParams(vmem_limit_bytes=VMEM_LIMIT),
        name="attend",
    )(meta, start, queries, keys, values, keys_b, values_b)


def split3(row):
    high = row.astype(BF16).astype(F32)
    rest = row - high
    middle = rest.astype(BF16).astype(F32)
    return high, middle, rest - middle


def finish_kernel(
    chips, layers, msg_ref, w_ref, att_ref, z_ref,
    w, in_msg, own_chunk, gathered, natural, terms,
    local_sems, a_send, a_recv, g_send, g_recv, s_send, s_recv, z_send, z_recv,
):
    ctx = lax.axis_index("ctx")
    layer = lax.axis_index("kvh")
    chip, core = ctx // 2, lax.rem(ctx, 2)
    other = {"ctx": ctx + 1 - 2 * core}
    tokens_here, heads, _ = att_ref.shape
    pieces = msg_ref.shape[0]
    _, per_layer, width = z_ref.shape
    half_heads = heads // 2
    depth = half_heads * HD
    piece = chips * 64 // half_heads

    def extent(s):
        return pl.ds(0, 64 if s else 80)

    load_w = pltpu.make_async_copy(w_ref, w, local_sems.at[pieces])
    load_own = [
        pltpu.make_async_copy(msg_ref.at[s, chip, extent(s)], in_msg.at[s, chip, extent(s)], local_sems.at[s])
        for s in range(pieces)
    ]
    peers = [partner(chip, chips, step) for step in steps(chips)]
    far_layers = sorted(range(1, layers), key=lambda k: -min(k, layers - k))
    greet_start(
        [{"ctx": peer * 2 + core} for peer in peers]
        + [{"kvh": lax.rem(layer + k, layers)} for k in far_layers]
        + [other]
    )
    for copy in load_own:
        copy.start()
    load_w.start()
    pl.semaphore_wait(pltpu.get_barrier_semaphore(), chips + layers - 1)

    for s in range(pieces):
        for peer in peers:
            remote(
                msg_ref.at[s, peer, extent(s)], in_msg.at[s, chip, extent(s)], a_send.at[s], a_recv.at[s],
                {"ctx": peer * 2 + core},
            ).start()
    pad = jnp.zeros((128 - chips, 128), F32)
    rest = pl.ds(0, chips - 1)

    def combine(s):
        load_own[s].wait()
        landed(in_msg.at[s, rest, extent(s)], a_recv.at[s])
        tops_in, totals_in = [], []
        for source in range(chips):
            lines = in_msg[0, source, 64:80, :].astype(F32)[6 * s : 6 * s + 6]
            tops_in.append(lines[0:1] + lines[1:2] + lines[2:3])
            totals_in.append(lines[3:4] + lines[4:5] + lines[5:6])
        top = jnp.concatenate(tops_in, axis=0)
        scale = jnp.exp2(top - jnp.max(top, axis=0, keepdims=True))
        total = jnp.sum(scale * jnp.concatenate(totals_in, axis=0), axis=0, keepdims=True)
        turned = jnp.concatenate([scale / total, pad], axis=0).T
        attention = jnp.zeros((64, HD), F32)
        for source in range(chips):
            attention = attention + turned[0:64, source : source + 1] * in_msg[s, source, 0:64, :].astype(F32)
        own_chunk[s] = attention.astype(BF16)
        gathered[s, core, chip] = own_chunk[s]

    def pair_copy(s):
        return remote(gathered.at[s, core], gathered.at[s, core], s_send.at[s], s_recv.at[s], other)

    def product(s, which):
        block = gathered[s, which].reshape(half_heads, piece, HD)
        columns = [block[head] for head in range(half_heads)]
        rows = pl.ds(pl.multiple_of(which * depth, depth), depth)
        return jnp.dot(jnp.concatenate(columns, axis=1), w[rows, :], preferred_element_type=F32)

    for s in range(pieces):
        combine(s)
        for peer in peers:
            remote(
                own_chunk.at[s], gathered.at[s, core, chip], g_send.at[s], g_recv.at[s], {"ctx": peer * 2 + core}
            ).start()
    load_w.wait()
    for s in range(pieces):
        landed(gathered.at[s, core, rest], g_recv.at[s])
        pair_copy(s).start()
        held = product(s, core)
        landed(gathered.at[s, 1 - core], s_recv.at[s])
        ready = (held + product(s, 1 - core)).astype(BF16).reshape(layers // pieces, per_layer, width)
        for j in range(layers // pieces):
            terms[pieces * j + s] = ready[j]
        nearest = layer + lax.rem(layer + s, pieces)
        for k in sorted(range(0, layers, pieces), key=lambda k: -min(k, layers - k)):
            target = lax.rem(nearest + k, layers)

            @pl.when(layer != target)
            def _(target=target):
                remote(terms.at[target], z_ref.at[layer], z_send, z_recv, {"kvh": target}).start()

    keep = pltpu.make_async_copy(terms.at[layer], z_ref.at[layer], local_sems.at[0])
    keep.start()

    two = 2 * tokens_here
    block = chip * two // per_layer
    line = block // pieces * per_layer + lax.rem(chip * two, per_layer)
    for head in range(heads):
        flat = head % half_heads * piece + line
        rows = pl.ds(pl.multiple_of(lax.rem(flat, 64), two), two)
        both = gathered[lax.rem(block, pieces), head // half_heads, flat // 64, rows, :].astype(F32)
        mine = jnp.where(core == 0, both[0:tokens_here], both[tokens_here:two])
        natural[pl.ds(head, tokens_here, stride=heads), :] = mine
    att_ref[...] = natural[...].astype(BF16).reshape(att_ref.shape)

    for s in range(pieces):
        landed(in_msg.at[s, rest, extent(s)], a_send.at[s])
        landed(gathered.at[s, core, rest], g_send.at[s])
        pair_copy(s).wait_send()
    keep.wait()
    layers_rest = z_ref.at[pl.ds(0, layers - 1)]
    landed(layers_rest, z_send)
    landed(layers_rest, z_recv)


def finish(mesh, messages, out_weight, tokens_here):
    chips, layers = mesh.shape["ctx"] // 2, mesh.shape["kvh"]
    width = out_weight.shape[1]
    tokens = chips * 2 * tokens_here
    dma = pltpu.SemaphoreType.DMA
    vmem = pl.BlockSpec(memory_space=pltpu.VMEM)
    anywhere = pl.BlockSpec(memory_space=pl.ANY)
    pieces = messages.shape[0]
    return pl.pallas_call(
        functools.partial(finish_kernel, chips, layers),
        out_shape=(
            jax.ShapeDtypeStruct((tokens_here, HEADS_HERE, HD), BF16),
            jax.ShapeDtypeStruct((layers, tokens // layers, width), BF16),
        ),
        in_specs=[anywhere] * 2,
        out_specs=(vmem, anywhere),
        scratch_shapes=[
            pltpu.VMEM(out_weight.shape, BF16),
            pltpu.VMEM(messages.shape, BF16),
            pltpu.VMEM((pieces, 64, HD), BF16),
            pltpu.VMEM((pieces, 2, chips, 64, HD), BF16),
            pltpu.VMEM((HEADS_HERE * tokens_here, HD), F32),
            pltpu.VMEM((layers, tokens // layers, width), BF16),
            dma((pieces + 1,)),
            dma((pieces,)),
            dma((pieces,)),
            dma((pieces,)),
            dma((pieces,)),
            dma((pieces,)),
            dma((pieces,)),
            dma,
            dma,
        ],
        compiler_params=pltpu.CompilerParams(
            collective_id=1, has_side_effects=True, vmem_limit_bytes=VMEM_LIMIT
        ),
        name="finish",
    )(messages, out_weight)


def total_kernel(att_ref, z_ref, att_out, proj_out):
    att_out[...] = att_ref[...]
    projected = z_ref[0].astype(F32)
    for source in range(1, z_ref.shape[0]):
        projected = projected + z_ref[source].astype(F32)
    proj_out[...] = projected.astype(BF16)


def total(attention, terms):
    vmem = pl.BlockSpec(memory_space=pltpu.VMEM)
    return pl.pallas_call(
        total_kernel,
        out_shape=(
            jax.ShapeDtypeStruct(attention.shape, BF16),
            jax.ShapeDtypeStruct(terms.shape[1:], BF16),
        ),
        in_specs=[vmem] * 2,
        out_specs=(vmem, vmem),
        compiler_params=pltpu.CompilerParams(vmem_limit_bytes=VMEM_LIMIT),
        name="total",
    )(attention, terms)


def solution(mesh, chunk=512):
    def local(queries, key_cache, value_cache, block_lengths, block_home, stretch_start, out_weight):
        slots = key_cache.shape[0]
        keys, values = key_cache.reshape(slots, HD), value_cache.reshape(slots, HD)
        qall, keys_b, values_b, meta = gather_queries(mesh, queries, block_lengths, block_home, keys, values)
        messages = attend(qall, keys, values, keys_b, values_b, meta, stretch_start, mesh.shape["kvh"], chunk)
        return total(*finish(mesh, messages, out_weight, queries.shape[0]))

    in_specs = (
        P("ctx", "kvh", None),
        P("ctx", "kvh", None),
        P("ctx", "kvh", None),
        P(),
        P(),
        P(),
        P("kvh", "ctx"),
    )
    out_specs = (P("ctx", "kvh", None), P("kvh", "ctx"))
    return jax.shard_map(local, mesh=mesh, in_specs=in_specs, out_specs=out_specs, check_vma=False)
```

```python
import functools
import math

import jax
import jax.numpy as jnp
from jax import lax
from jax.experimental import pallas as pl
from jax.experimental.pallas import tpu as pltpu
from jax.sharding import PartitionSpec as P

HD = 128
PAGE = 256
HEADS_HERE = 16
SUB = 256
GROUP = 3
NEG = -1e30
FAR = 1 << 30
LOG2E_SCALE = math.log2(math.e) / math.sqrt(HD)
F32 = jnp.float32
BF16 = jnp.bfloat16
VMEM_LIMIT = 56 * 1024 * 1024


def greet_start(devices):
    for device in devices:
        pl.semaphore_signal(
            pltpu.get_barrier_semaphore(), inc=1, device_id=device, device_id_type=pl.DeviceIdType.MESH
        )


def remote(src, dst, send, recv, device):
    return pltpu.make_async_remote_copy(
        src_ref=src,
        dst_ref=dst,
        send_sem=send,
        recv_sem=recv,
        device_id=device,
        device_id_type=pl.DeviceIdType.MESH,
    )


def loop(start, stop, body):
    def step(k, _):
        body(k)
        return 0

    lax.fori_loop(start, stop, step, 0)


def partner(chip, chips, step):
    if chips != 16:
        return lax.rem(chip + step, chips)
    return lax.rem(chip // 4 + step // 4, 4) * 4 + lax.rem(chip + step, 4)


def steps(chips):
    if chips != 16:
        return list(range(1, chips))
    near = [0, 1, 2, 1]
    return sorted(range(1, chips), key=lambda step: -(near[step // 4] + near[step % 4]))


def landed(buffer, sem):
    pltpu.make_async_copy(buffer, buffer, sem).wait()


def gather_kernel(
    devices, q_ref, len_ref, home_ref, k_ref, v_ref, qall_ref, k_out, v_out, meta_ref,
    q_in, len_in, home_in, mine, natural, send, recv, kv_send, kv_recv, own_sem, in_sems,
):
    ctx = lax.axis_index("ctx")
    core = lax.rem(ctx, 2)
    other = {"ctx": ctx + 1 - 2 * core}
    tokens, heads = q_ref.shape[0], q_ref.shape[1]
    half = heads // 2
    loads = [
        pltpu.make_async_copy(source, target, in_sems.at[i])
        for i, (source, target) in enumerate([(q_ref, q_in), (len_ref, len_in), (home_ref, home_in)])
    ]
    for load in loads:
        load.start()
    chip, chips = ctx // 2, devices // 2
    peers = [partner(chip, chips, step) * 2 + side for step in steps(chips) for side in range(2)]
    peers.append(ctx + 1 - 2 * core)
    greet_start([{"ctx": peer} for peer in peers])
    loads[0].wait()
    natural[...] = q_in[...].astype(F32).reshape(tokens * heads, HD)
    for part in range(2):
        rows = [natural[pl.ds(part * half + head, tokens, stride=heads), :] for head in range(half)]
        mine[part] = jnp.concatenate(rows, axis=0).astype(BF16)
    pl.semaphore_wait(pltpu.get_barrier_semaphore(), devices - 1)

    for peer in peers:
        remote(mine.at[lax.rem(peer, 2)], qall_ref.at[ctx], send, recv, {"ctx": peer}).start()
    own = pltpu.make_async_copy(mine.at[core], qall_ref.at[ctx], own_sem)
    own.start()
    pairs = [
        remote(k_ref, k_out, kv_send.at[0], kv_recv.at[0], other),
        remote(v_ref, v_out, kv_send.at[1], kv_recv.at[1], other),
    ]
    for pair in pairs:
        pair.start()

    pages, blocks = meta_ref.shape[0], home_ref.shape[1]
    loads[1].wait()
    loads[2].wait()
    lengths = len_in[...].astype(F32)
    index = lax.broadcasted_iota(jnp.int32, (pages, blocks), 0)
    here = pages // 2
    stored = jnp.where(index < here, ctx * here + index, (ctx + 1 - 2 * core) * here + index - here)
    logical = lax.broadcasted_iota(jnp.int32, (pages, blocks), 1).astype(F32)
    match = home_in[...] == stored
    place = jnp.sum(jnp.where(match, logical, 0.0), axis=1, keepdims=True)
    filled = jnp.sum(jnp.where(match, lengths, 0.0), axis=1, keepdims=True)
    begin = jnp.sum(jnp.where(logical < place, lengths, 0.0), axis=1, keepdims=True)
    lane = lax.broadcasted_iota(jnp.int32, (pages, 128), 1)
    meta = jnp.where(lane == 0, begin, jnp.where(lane == 1, filled, 0.0))
    meta_ref[...] = meta.astype(jnp.int32)

    own.wait()

    others = qall_ref.at[pl.ds(0, devices - 1)]
    landed(others, recv)
    for pair in pairs:
        pair.wait()
    landed(others, send)


def gather_queries(mesh, queries, block_lengths, block_home, keys, values):
    devices = mesh.shape["ctx"]
    tokens, heads, _ = queries.shape
    rows = tokens * heads // 2
    pages = 2 * keys.shape[0] // PAGE
    dma = pltpu.SemaphoreType.DMA
    vmem = pl.BlockSpec(memory_space=pltpu.VMEM)
    anywhere = pl.BlockSpec(memory_space=pl.ANY)
    return pl.pallas_call(
        functools.partial(gather_kernel, devices),
        out_shape=(
            jax.ShapeDtypeStruct((devices, rows, HD), BF16),
            jax.ShapeDtypeStruct(keys.shape, BF16),
            jax.ShapeDtypeStruct(values.shape, BF16),
            jax.ShapeDtypeStruct((pages, 128), jnp.int32),
        ),
        in_specs=[anywhere] * 5,
        out_specs=(anywhere, anywhere, anywhere, vmem),
        scratch_shapes=[
            pltpu.VMEM(queries.shape, BF16),
            pltpu.VMEM((1, block_lengths.shape[0]), jnp.int32),
            pltpu.VMEM((1, block_home.shape[0]), jnp.int32),
            pltpu.VMEM((2, rows, HD), BF16),
            pltpu.VMEM((2 * rows, HD), F32),
            dma,
            dma,
            dma((2,)),
            dma((2,)),
            dma,
            dma((3,)),
        ],
        compiler_params=pltpu.CompilerParams(
            collective_id=0, has_side_effects=True, vmem_limit_bytes=VMEM_LIMIT
        ),
        name="gather_queries",
    )(queries, block_lengths.reshape(1, -1), block_home.reshape(1, -1), keys, values)


def attend_kernel(
    chunk, layers,
    meta_ref, start_ref, q_ref, k_a, v_a, k_b, v_b, msg_ref,
    q_in, q_sem, k_in, v_in, k_sem, v_sem, kc, vc, qh, bias, scores, peaks, tops, sums, tail, base_ref,
):
    pages = meta_ref.shape[0]
    pieces, heads, piece, _ = qh.shape
    devices = q_ref.shape[0]
    tile = heads * piece
    tokens = pieces * piece
    tokens_here = tokens // devices
    two = 2 * tokens_here
    per_layer = tokens // layers
    first = start_ref[0]
    last = first + tokens - 1
    slot = lax.broadcasted_iota(jnp.int32, (PAGE, HD), 0)
    here = pages // 2

    def fetch(page, keys, values):
        source = pl.ds(pl.multiple_of(lax.rem(page, here) * PAGE, PAGE), PAGE)
        return (
            pltpu.make_async_copy(keys.at[source, :], k_in.at[page], k_sem.at[page]),
            pltpu.make_async_copy(values.at[source, :], v_in.at[page], v_sem.at[page]),
        )

    def request(page, keys, values):
        @pl.when(meta_ref[page, 0] <= last)
        def _():
            for copy in fetch(page, keys, values):
                copy.start()

    load_q = pltpu.make_async_copy(q_ref, q_in, q_sem)
    load_q.start()
    loop(0, here, lambda p: request(p, k_a, v_a))
    loop(here, pages, lambda p: request(p, k_b, v_b))

    def arrange(chip):
        block = q_in[pl.ds(2 * chip, 2)].astype(F32).reshape(2, heads, tokens_here, HD)
        layer = chip * two // per_layer
        line = layer // pieces * per_layer + lax.rem(chip * two, per_layer)
        target = pl.ds(pl.multiple_of(line, two), two)
        for head in range(heads):
            rows = jnp.concatenate([block[0, head], block[1, head]], axis=0)
            qh[lax.rem(layer, pieces), head, target, :] = rows.astype(BF16)

    def visit(page, used, masked):
        begin, filled = meta_ref[page, 0], meta_ref[page, 1]
        partly = begin + filled - 1 > first
        seen = begin <= last
        take = jnp.logical_and(seen, partly) if masked else jnp.logical_not(partly)

        @pl.when(take)
        def _():
            base_ref[page] = used
            target = pl.ds(pl.multiple_of(used, 16), PAGE)
            for copy in fetch(page, k_a, v_a):
                copy.wait()
            keys = k_in[page].astype(F32)
            live = slot < filled
            lead = jnp.broadcast_to(keys[0:1, :], (PAGE, HD))
            kc[target, :] = jnp.where(live, keys, lead).astype(BF16)
            tail[...] = lead[0:16, :].astype(BF16)
            values = v_in[page].astype(F32)
            vc[target, 0:HD] = jnp.where(live, values, 0.0).astype(BF16)
            vc[target, HD : 2 * HD] = jnp.where(live, 1.0, 0.0).astype(BF16)

        if not masked:

            @pl.when(jnp.logical_not(take))
            def _():
                base_ref[page] = FAR

        return used + jnp.where(take, (filled + 15) // 16 * 16, 0)

    tail[...] = jnp.zeros_like(tail)
    plain = lax.fori_loop(0, pages, lambda p, u: visit(p, u, False), jnp.int32(0))
    used = lax.fori_loop(0, pages, lambda p, u: visit(p, u, True), plain)
    for part in range(chunk // 16):
        target = pl.ds(pl.multiple_of(used + part * 16, 16), 16)
        kc[target, :] = tail[...]
        vc[target, :] = jnp.zeros((16, 2 * HD), BF16)
    load_q.wait()
    loop(0, devices // 2, arrange)
    chunks = (used + chunk - 1) // chunk
    clear = jnp.where(used > plain, plain // chunk, chunks)
    per_part = SUB // piece
    parts = tile // SUB

    def shade(position):
        index = position * chunk + lax.broadcasted_iota(jnp.int32, (1, chunk), 1)

        def mark(page, key_pos):
            base = base_ref[page]
            inside = jnp.logical_and(index >= base, index < base + meta_ref[page, 1])
            return jnp.where(inside, index - base + meta_ref[page, 0], key_pos)

        key_pos = lax.fori_loop(0, pages, mark, jnp.full((1, chunk), FAR, jnp.int32))
        line = lax.broadcasted_iota(jnp.int32, (piece, 1), 0)
        for s in range(pieces):
            token = (line // per_layer * pieces + s) * per_layer + lax.rem(line, per_layer)
            bias[s, position] = jnp.where(key_pos <= first + token, 0.0, NEG).astype(BF16)

    loop(clear, chunks, shade)

    def score(tile_index, position, masked, part):
        q = qh[tile_index, part * per_part : (part + 1) * per_part].reshape(SUB, HD)
        keys = kc[pl.ds(pl.multiple_of(position * chunk, chunk), chunk), :]
        s = lax.dot_general(q, keys, (((1,), (1,)), ((), ())), preferred_element_type=F32)
        if masked:
            shadow = bias[tile_index, position].astype(F32)
            s = s + jnp.concatenate([shadow] * per_part, axis=0)
        rows = pl.ds(part * SUB, SUB)
        scores[position, rows, :] = s
        peak = peaks[rows, :]
        for group in range(chunk // 128):
            peak = jnp.maximum(peak, s[:, group * 128 : (group + 1) * 128])
        peaks[rows, :] = peak

    def mix(position, part):
        rows = pl.ds(part * SUB, SUB)
        top = tops[rows, :]
        weights = []
        for group in range(chunk // 128):
            s = scores[position, rows, group * 128 : (group + 1) * 128]
            weights.append(jnp.exp2((s - top) * LOG2E_SCALE).astype(BF16))
        values = vc[pl.ds(pl.multiple_of(position * chunk, chunk), chunk), :]
        sums[rows, :] += jnp.dot(jnp.concatenate(weights, axis=1), values, preferred_element_type=F32)

    def settle():
        tops[...] = jnp.broadcast_to(jnp.max(peaks[...], axis=1, keepdims=True), (tile, 128))

    sub = lax.broadcasted_iota(jnp.int32, (16, 128), 0)
    lane = lax.broadcasted_iota(jnp.int32, (128, 128), 1)
    blocks = tile // 128

    def finish(tile_index):
        packed = jnp.zeros((128, 128), F32)
        for block in range(blocks):
            rows = pl.ds(block * 128, 128)
            packed = jnp.where(lane == block, tops[rows, :] * LOG2E_SCALE, packed)
            packed = jnp.where(lane == blocks + block, sums[rows, HD : 2 * HD], packed)
            for part in range(2):
                lines = pl.ds(block * 128 + part * 64, 64)
                msg_ref[tile_index, 2 * block + part, 0:64, :] = sums[lines, 0:HD].astype(BF16)
        stats = packed.T
        for block in range(blocks):
            lines = jnp.zeros((16, 128), F32)
            if tile_index:
                lines = msg_ref[0, 2 * block, 64:80, :].astype(F32)
            values = split3(stats[block : block + 1]) + split3(stats[blocks + block : blocks + block + 1])
            for line, value in enumerate(values):
                lines = jnp.where(sub == 6 * tile_index + line, jnp.broadcast_to(value, (16, 128)), lines)
            msg_ref[0, 2 * block, 64:80, :] = lines.astype(BF16)
            turned = jnp.concatenate([lines[:, 64:128], lines[:, 0:64]], axis=1)
            msg_ref[0, 2 * block + 1, 64:80, :] = turned.astype(BF16)

    def grouped(count, step):
        def turn(i):
            for k in range(GROUP):
                step(GROUP * i + k)

        loop(0, count // GROUP, turn)
        loop(count // GROUP * GROUP, count, step)

    def over_chunks(step):
        grouped(clear, lambda c: step(c, False))
        loop(clear, chunks, lambda c: step(c, True))

    def score_all(c, masked):
        for part in range(parts):
            score(0, c, masked, part)

    peaks[...] = jnp.full_like(peaks, NEG)
    over_chunks(score_all)
    settle()

    for t in range(1, pieces):
        peaks[...] = jnp.full_like(peaks, NEG)
        sums[...] = jnp.zeros_like(sums)

        def both(c, masked, t=t):
            for part in range(parts):
                mix(c, part)
                score(t, c, masked, part)

        over_chunks(both)
        finish(t - 1)
        settle()

    def mix_all(c):
        for part in range(parts):
            mix(c, part)

    sums[...] = jnp.zeros_like(sums)
    grouped(chunks, mix_all)
    finish(pieces - 1)


def attend(queries, keys, values, keys_b, values_b, meta, start, layers, chunk):
    devices, rows, _ = queries.shape
    pages = meta.shape[0]
    slots = pages * PAGE
    heads = HEADS_HERE // 2
    pieces = 2
    piece = devices * rows // (heads * pieces)
    tile = heads * piece
    dma = pltpu.SemaphoreType.DMA
    vmem = pl.BlockSpec(memory_space=pltpu.VMEM)
    smem = pl.BlockSpec(memory_space=pltpu.SMEM)
    anywhere = pl.BlockSpec(memory_space=pl.ANY)
    return pl.pallas_call(
        functools.partial(attend_kernel, chunk, layers),
        out_shape=jax.ShapeDtypeStruct((pieces, devices // 2, 80, HD), BF16),
        in_specs=[smem, smem] + [anywhere] * 5,
        out_specs=vmem,
        scratch_shapes=[
            pltpu.VMEM(queries.shape, BF16),
            dma,
            pltpu.VMEM((pages, PAGE, HD), BF16),
            pltpu.VMEM((pages, PAGE, HD), BF16),
            dma((pages,)),
            dma((pages,)),
            pltpu.VMEM((slots + chunk, HD), BF16),
            pltpu.VMEM((slots + chunk, 2 * HD), BF16),
            pltpu.VMEM((pieces, heads, piece, HD), BF16),
            pltpu.VMEM((pieces, slots // chunk, piece, chunk), BF16),
            pltpu.VMEM((slots // chunk, tile, chunk), F32),
            pltpu.VMEM((tile, 128), F32),
            pltpu.VMEM((tile, 128), F32),
            pltpu.VMEM((tile, 2 * HD), F32),
            pltpu.VMEM((16, HD), BF16),
            pltpu.SMEM((pages,), jnp.int32),
        ],
        compiler_params=pltpu.CompilerParams(vmem_limit_bytes=VMEM_LIMIT),
        name="attend",
    )(meta, start, queries, keys, values, keys_b, values_b)


def split3(row):
    high = row.astype(BF16).astype(F32)
    rest = row - high
    middle = rest.astype(BF16).astype(F32)
    return high, middle, rest - middle


def finish_kernel(
    chips, layers, msg_ref, w_ref, att_ref, z_ref,
    w, in_msg, own_chunk, gathered, natural, terms,
    local_sems, a_send, a_recv, g_send, g_recv, s_send, s_recv, z_send, z_recv,
):
    ctx = lax.axis_index("ctx")
    layer = lax.axis_index("kvh")
    chip, core = ctx // 2, lax.rem(ctx, 2)
    other = {"ctx": ctx + 1 - 2 * core}
    tokens_here, heads, _ = att_ref.shape
    pieces = msg_ref.shape[0]
    _, per_layer, width = z_ref.shape
    half_heads = heads // 2
    depth = half_heads * HD
    piece = chips * 64 // half_heads

    def extent(s):
        return pl.ds(0, 64 if s else 80)

    load_w = pltpu.make_async_copy(w_ref, w, local_sems.at[pieces])
    load_own = [
        pltpu.make_async_copy(msg_ref.at[s, chip, extent(s)], in_msg.at[s, chip, extent(s)], local_sems.at[s])
        for s in range(pieces)
    ]
    peers = [partner(chip, chips, step) for step in steps(chips)]
    far_layers = sorted(range(1, layers), key=lambda k: -min(k, layers - k))
    greet_start(
        [{"ctx": peer * 2 + core} for peer in peers]
        + [{"kvh": lax.rem(layer + k, layers)} for k in far_layers]
        + [other]
    )
    for copy in load_own:
        copy.start()
    load_w.start()
    pl.semaphore_wait(pltpu.get_barrier_semaphore(), chips + layers - 1)

    for s in range(pieces):
        for peer in peers:
            remote(
                msg_ref.at[s, peer, extent(s)], in_msg.at[s, chip, extent(s)], a_send.at[s], a_recv.at[s],
                {"ctx": peer * 2 + core},
            ).start()
    pad = jnp.zeros((128 - chips, 128), F32)
    rest = pl.ds(0, chips - 1)

    def combine(s):
        load_own[s].wait()
        landed(in_msg.at[s, rest, extent(s)], a_recv.at[s])
        tops_in, totals_in = [], []
        for source in range(chips):
            lines = in_msg[0, source, 64:80, :].astype(F32)[6 * s : 6 * s + 6]
            tops_in.append(lines[0:1] + lines[1:2] + lines[2:3])
            totals_in.append(lines[3:4] + lines[4:5] + lines[5:6])
        top = jnp.concatenate(tops_in, axis=0)
        scale = jnp.exp2(top - jnp.max(top, axis=0, keepdims=True))
        total = jnp.sum(scale * jnp.concatenate(totals_in, axis=0), axis=0, keepdims=True)
        turned = jnp.concatenate([scale / total, pad], axis=0).T
        attention = jnp.zeros((64, HD), F32)
        for source in range(chips):
            attention = attention + turned[0:64, source : source + 1] * in_msg[s, source, 0:64, :].astype(F32)
        own_chunk[s] = attention.astype(BF16)
        gathered[s, core, chip] = own_chunk[s]

    def pair_copy(s):
        return remote(gathered.at[s, core], gathered.at[s, core], s_send.at[s], s_recv.at[s], other)

    def product(s, which):
        block = gathered[s, which].reshape(half_heads, piece, HD)
        columns = [block[head] for head in range(half_heads)]
        rows = pl.ds(pl.multiple_of(which * depth, depth), depth)
        return jnp.dot(jnp.concatenate(columns, axis=1), w[rows, :], preferred_element_type=F32)

    for s in range(pieces):
        combine(s)
        for peer in peers:
            remote(
                own_chunk.at[s], gathered.at[s, core, chip], g_send.at[s], g_recv.at[s], {"ctx": peer * 2 + core}
            ).start()
    load_w.wait()
    for s in range(pieces):
        landed(gathered.at[s, core, rest], g_recv.at[s])
        pair_copy(s).start()
        held = product(s, core)
        landed(gathered.at[s, 1 - core], s_recv.at[s])
        ready = (held + product(s, 1 - core)).astype(BF16).reshape(layers // pieces, per_layer, width)
        for j in range(layers // pieces):
            terms[pieces * j + s] = ready[j]
        nearest = layer + lax.rem(layer + s, pieces)
        for k in sorted(range(0, layers, pieces), key=lambda k: -min(k, layers - k)):
            target = lax.rem(nearest + k, layers)

            @pl.when(layer != target)
            def _(target=target):
                remote(terms.at[target], z_ref.at[layer], z_send, z_recv, {"kvh": target}).start()

    keep = pltpu.make_async_copy(terms.at[layer], z_ref.at[layer], local_sems.at[0])
    keep.start()

    two = 2 * tokens_here
    block = chip * two // per_layer
    line = block // pieces * per_layer + lax.rem(chip * two, per_layer)
    for head in range(heads):
        flat = head % half_heads * piece + line
        rows = pl.ds(pl.multiple_of(lax.rem(flat, 64), two), two)
        both = gathered[lax.rem(block, pieces), head // half_heads, flat // 64, rows, :].astype(F32)
        mine = jnp.where(core == 0, both[0:tokens_here], both[tokens_here:two])
        natural[pl.ds(head, tokens_here, stride=heads), :] = mine
    att_ref[...] = natural[...].astype(BF16).reshape(att_ref.shape)

    for s in range(pieces):
        landed(in_msg.at[s, rest, extent(s)], a_send.at[s])
        landed(gathered.at[s, core, rest], g_send.at[s])
        pair_copy(s).wait_send()
    keep.wait()
    layers_rest = z_ref.at[pl.ds(0, layers - 1)]
    landed(layers_rest, z_send)
    landed(layers_rest, z_recv)


def finish(mesh, messages, out_weight, tokens_here):
    chips, layers = mesh.shape["ctx"] // 2, mesh.shape["kvh"]
    width = out_weight.shape[1]
    tokens = chips * 2 * tokens_here
    dma = pltpu.SemaphoreType.DMA
    vmem = pl.BlockSpec(memory_space=pltpu.VMEM)
    anywhere = pl.BlockSpec(memory_space=pl.ANY)
    pieces = messages.shape[0]
    return pl.pallas_call(
        functools.partial(finish_kernel, chips, layers),
        out_shape=(
            jax.ShapeDtypeStruct((tokens_here, HEADS_HERE, HD), BF16),
            jax.ShapeDtypeStruct((layers, tokens // layers, width), BF16),
        ),
        in_specs=[anywhere] * 2,
        out_specs=(vmem, anywhere),
        scratch_shapes=[
            pltpu.VMEM(out_weight.shape, BF16),
            pltpu.VMEM(messages.shape, BF16),
            pltpu.VMEM((pieces, 64, HD), BF16),
            pltpu.VMEM((pieces, 2, chips, 64, HD), BF16),
            pltpu.VMEM((HEADS_HERE * tokens_here, HD), F32),
            pltpu.VMEM((layers, tokens // layers, width), BF16),
            dma((pieces + 1,)),
            dma((pieces,)),
            dma((pieces,)),
            dma((pieces,)),
            dma((pieces,)),
            dma((pieces,)),
            dma((pieces,)),
            dma,
            dma,
        ],
        compiler_params=pltpu.CompilerParams(
            collective_id=1, has_side_effects=True, vmem_limit_bytes=VMEM_LIMIT
        ),
        name="finish",
    )(messages, out_weight)


def total_kernel(att_ref, z_ref, att_out, proj_out):
    att_out[...] = att_ref[...]
    projected = z_ref[0].astype(F32)
    for source in range(1, z_ref.shape[0]):
        projected = projected + z_ref[source].astype(F32)
    proj_out[...] = projected.astype(BF16)


def total(attention, terms):
    vmem = pl.BlockSpec(memory_space=pltpu.VMEM)
    return pl.pallas_call(
        total_kernel,
        out_shape=(
            jax.ShapeDtypeStruct(attention.shape, BF16),
            jax.ShapeDtypeStruct(terms.shape[1:], BF16),
        ),
        in_specs=[vmem] * 2,
        out_specs=(vmem, vmem),
        compiler_params=pltpu.CompilerParams(vmem_limit_bytes=VMEM_LIMIT),
        name="total",
    )(attention, terms)


def solution(mesh, chunk=512):
    def local(queries, key_cache, value_cache, block_lengths, block_home, stretch_start, out_weight):
        slots = key_cache.shape[0]
        keys, values = key_cache.reshape(slots, HD), value_cache.reshape(slots, HD)
        qall, keys_b, values_b, meta = gather_queries(mesh, queries, block_lengths, block_home, keys, values)
        messages = attend(qall, keys, values, keys_b, values_b, meta, stretch_start, mesh.shape["kvh"], chunk)
        return total(*finish(mesh, messages, out_weight, queries.shape[0]))

    in_specs = (
        P("ctx", "kvh", None),
        P("ctx", "kvh", None),
        P("ctx", "kvh", None),
        P(),
        P(),
        P(),
        P("kvh", "ctx"),
    )
    out_specs = (P("ctx", "kvh", None), P("kvh", "ctx"))
    return jax.shard_map(local, mesh=mesh, in_specs=in_specs, out_specs=out_specs, check_vma=False)
```

```python
import functools
import math

import jax
import jax.numpy as jnp
from jax import lax
from jax.experimental import pallas as pl
from jax.experimental.pallas import tpu as pltpu
from jax.sharding import PartitionSpec as P

HD = 128
PAGE = 256
HEADS_HERE = 16
SUB = 256
GROUP = 3
NEG = -1e30
FAR = 1 << 30
LOG2E_SCALE = math.log2(math.e) / math.sqrt(HD)
F32 = jnp.float32
BF16 = jnp.bfloat16
VMEM_LIMIT = 56 * 1024 * 1024


def greet_start(devices):
    for device in devices:
        pl.semaphore_signal(
            pltpu.get_barrier_semaphore(), inc=1, device_id=device, device_id_type=pl.DeviceIdType.MESH
        )


def remote(src, dst, send, recv, device):
    return pltpu.make_async_remote_copy(
        src_ref=src,
        dst_ref=dst,
        send_sem=send,
        recv_sem=recv,
        device_id=device,
        device_id_type=pl.DeviceIdType.MESH,
    )


def loop(start, stop, body):
    def step(k, _):
        body(k)
        return 0

    lax.fori_loop(start, stop, step, 0)


def partner(chip, chips, step):
    if chips != 16:
        return lax.rem(chip + step, chips)
    return lax.rem(chip // 4 + step // 4, 4) * 4 + lax.rem(chip + step, 4)


def steps(chips):
    if chips != 16:
        return list(range(1, chips))
    near = [0, 1, 2, 1]
    return sorted(range(1, chips), key=lambda step: -(near[step // 4] + near[step % 4]))


def landed(buffer, sem):
    pltpu.make_async_copy(buffer, buffer, sem).wait()


def gather_kernel(
    devices, q_ref, len_ref, home_ref, k_ref, v_ref, qall_ref, k_out, v_out, meta_ref,
    q_in, len_in, home_in, mine, natural, send, recv, kv_send, kv_recv, own_sem, in_sems,
):
    ctx = lax.axis_index("ctx")
    core = lax.rem(ctx, 2)
    other = {"ctx": ctx + 1 - 2 * core}
    tokens, heads = q_ref.shape[0], q_ref.shape[1]
    half = heads // 2
    loads = [
        pltpu.make_async_copy(source, target, in_sems.at[i])
        for i, (source, target) in enumerate([(q_ref, q_in), (len_ref, len_in), (home_ref, home_in)])
    ]
    for load in loads:
        load.start()
    chip, chips = ctx // 2, devices // 2
    peers = [partner(chip, chips, step) * 2 + side for step in steps(chips) for side in range(2)]
    peers.append(ctx + 1 - 2 * core)
    greet_start([{"ctx": peer} for peer in peers])
    loads[0].wait()
    natural[...] = q_in[...].astype(F32).reshape(tokens * heads, HD)
    for part in range(2):
        rows = [natural[pl.ds(part * half + head, tokens, stride=heads), :] for head in range(half)]
        mine[part] = jnp.concatenate(rows, axis=0).astype(BF16)
    pl.semaphore_wait(pltpu.get_barrier_semaphore(), devices - 1)

    for peer in peers:
        remote(mine.at[lax.rem(peer, 2)], qall_ref.at[ctx], send, recv, {"ctx": peer}).start()
    own = pltpu.make_async_copy(mine.at[core], qall_ref.at[ctx], own_sem)
    own.start()
    pairs = [
        remote(k_ref, k_out, kv_send.at[0], kv_recv.at[0], other),
        remote(v_ref, v_out, kv_send.at[1], kv_recv.at[1], other),
    ]
    for pair in pairs:
        pair.start()

    pages, blocks = meta_ref.shape[0], home_ref.shape[1]
    loads[1].wait()
    loads[2].wait()
    lengths = len_in[...].astype(F32)
    index = lax.broadcasted_iota(jnp.int32, (pages, blocks), 0)
    here = pages // 2
    stored = jnp.where(index < here, ctx * here + index, (ctx + 1 - 2 * core) * here + index - here)
    logical = lax.broadcasted_iota(jnp.int32, (pages, blocks), 1).astype(F32)
    match = home_in[...] == stored
    place = jnp.sum(jnp.where(match, logical, 0.0), axis=1, keepdims=True)
    filled = jnp.sum(jnp.where(match, lengths, 0.0), axis=1, keepdims=True)
    begin = jnp.sum(jnp.where(logical < place, lengths, 0.0), axis=1, keepdims=True)
    lane = lax.broadcasted_iota(jnp.int32, (pages, 128), 1)
    meta = jnp.where(lane == 0, begin, jnp.where(lane == 1, filled, 0.0))
    meta_ref[...] = meta.astype(jnp.int32)

    own.wait()

    others = qall_ref.at[pl.ds(0, devices - 1)]
    landed(others, recv)
    for pair in pairs:
        pair.wait()
    landed(others, send)


def gather_queries(mesh, queries, block_lengths, block_home, keys, values):
    devices = mesh.shape["ctx"]
    tokens, heads, _ = queries.shape
    rows = tokens * heads // 2
    pages = 2 * keys.shape[0] // PAGE
    dma = pltpu.SemaphoreType.DMA
    vmem = pl.BlockSpec(memory_space=pltpu.VMEM)
    anywhere = pl.BlockSpec(memory_space=pl.ANY)
    return pl.pallas_call(
        functools.partial(gather_kernel, devices),
        out_shape=(
            jax.ShapeDtypeStruct((devices, rows, HD), BF16),
            jax.ShapeDtypeStruct(keys.shape, BF16),
            jax.ShapeDtypeStruct(values.shape, BF16),
            jax.ShapeDtypeStruct((pages, 128), jnp.int32),
        ),
        in_specs=[anywhere] * 5,
        out_specs=(anywhere, anywhere, anywhere, vmem),
        scratch_shapes=[
            pltpu.VMEM(queries.shape, BF16),
            pltpu.VMEM((1, block_lengths.shape[0]), jnp.int32),
            pltpu.VMEM((1, block_home.shape[0]), jnp.int32),
            pltpu.VMEM((2, rows, HD), BF16),
            pltpu.VMEM((2 * rows, HD), F32),
            dma,
            dma,
            dma((2,)),
            dma((2,)),
            dma,
            dma((3,)),
        ],
        compiler_params=pltpu.CompilerParams(
            collective_id=0, has_side_effects=True, vmem_limit_bytes=VMEM_LIMIT
        ),
        name="gather_queries",
    )(queries, block_lengths.reshape(1, -1), block_home.reshape(1, -1), keys, values)


def attend_kernel(
    chunk, layers,
    meta_ref, start_ref, q_ref, k_a, v_a, k_b, v_b, msg_ref,
    q_in, q_sem, k_in, v_in, k_sem, v_sem, kc, vc, where_at, vt, qh, scores, peaks, tops, sums, tail,
):
    pages = meta_ref.shape[0]
    pieces, heads, piece, _ = qh.shape
    devices = q_ref.shape[0]
    tile = heads * piece
    tokens = pieces * piece
    tokens_here = tokens // devices
    two = 2 * tokens_here
    per_layer = tokens // layers
    first = start_ref[0]
    last = first + tokens - 1
    slot = lax.broadcasted_iota(jnp.int32, (PAGE, HD), 0)
    here = pages // 2

    def fetch(page, keys, values):
        source = pl.ds(pl.multiple_of(lax.rem(page, here) * PAGE, PAGE), PAGE)
        return (
            pltpu.make_async_copy(keys.at[source, :], k_in.at[page], k_sem.at[page]),
            pltpu.make_async_copy(values.at[source, :], v_in.at[page], v_sem.at[page]),
        )

    def request(page, keys, values):
        @pl.when(meta_ref[page, 0] <= last)
        def _():
            for copy in fetch(page, keys, values):
                copy.start()

    load_q = pltpu.make_async_copy(q_ref, q_in, q_sem)
    load_q.start()
    loop(0, here, lambda p: request(p, k_a, v_a))
    loop(here, pages, lambda p: request(p, k_b, v_b))

    def arrange(chip):
        block = q_in[pl.ds(2 * chip, 2)].astype(F32).reshape(2, heads, tokens_here, HD)
        layer = chip * two // per_layer
        line = layer // pieces * per_layer + lax.rem(chip * two, per_layer)
        target = pl.ds(pl.multiple_of(line, two), two)
        for head in range(heads):
            rows = jnp.concatenate([block[0, head], block[1, head]], axis=0)
            qh[lax.rem(layer, pieces), head, target, :] = rows.astype(BF16)

    def visit(page, used, masked):
        begin, filled = meta_ref[page, 0], meta_ref[page, 1]
        partly = begin + filled - 1 > first
        seen = begin <= last
        take = jnp.logical_and(seen, partly) if masked else jnp.logical_not(partly)

        @pl.when(take)
        def _():
            target = pl.ds(pl.multiple_of(used, 16), PAGE)
            for copy in fetch(page, k_a, v_a):
                copy.wait()
            keys = k_in[page].astype(F32)
            live = slot < filled
            lead = jnp.broadcast_to(keys[0:1, :], (PAGE, HD))
            kc[target, :] = jnp.where(live, keys, lead).astype(BF16)
            tail[...] = lead[0:16, :].astype(BF16)
            vc[target, :] = jnp.where(live, v_in[page].astype(F32), 0.0)
            where_at[target, :] = jnp.where(live, begin + slot, FAR)

        return used + jnp.where(take, (filled + 15) // 16 * 16, 0)

    tail[...] = jnp.zeros_like(tail)
    plain = lax.fori_loop(0, pages, lambda p, u: visit(p, u, False), jnp.int32(0))
    used = lax.fori_loop(0, pages, lambda p, u: visit(p, u, True), plain)
    ending = pl.ds(pl.multiple_of(used, 16), chunk)
    kc[ending, :] = jnp.concatenate([tail[...]] * (chunk // 16), axis=0)
    vc[ending, :] = jnp.zeros((chunk, HD), F32)
    where_at[ending, :] = jnp.full((chunk, HD), FAR, jnp.int32)
    load_q.wait()
    loop(0, devices // 2, arrange)
    chunks = (used + chunk - 1) // chunk
    clear = jnp.where(used > plain, plain // chunk, chunks)
    per_part = SUB // piece
    parts = tile // SUB
    line = lax.broadcasted_iota(jnp.int32, (1, piece), 1)

    def span(position):
        return pl.ds(pl.multiple_of(position * chunk, chunk), chunk)

    def turn_values(position):
        vt[position, 0:HD, :] = vc[span(position), :].T.astype(BF16)
        live = jnp.where(where_at[span(position), :] < FAR, 1.0, 0.0).T
        vt[position, HD : HD + 16, :] = live[0:16, :].astype(BF16)

    def score(tile_index, position, masked, part):
        q = qh[tile_index, part * per_part : (part + 1) * per_part].reshape(SUB, HD)
        s = lax.dot_general(kc[span(position), :], q, (((1,), (1,)), ((), ())), preferred_element_type=F32)
        if masked:
            token = (line // per_layer * pieces + tile_index) * per_layer + lax.rem(line, per_layer)
            seen = where_at[span(position), 0:piece] <= first + token
            s = jnp.concatenate(
                [jnp.where(seen, s[:, head * piece : (head + 1) * piece], NEG) for head in range(per_part)], axis=1
            )
        across = slice(part * SUB, (part + 1) * SUB)
        scores[position, :, across] = s
        peaks[:, across] = jnp.maximum(peaks[:, across], jnp.max(s.reshape(chunk // 8, 8, SUB), axis=0))

    def mix(position, part):
        across = slice(part * SUB, (part + 1) * SUB)
        s = scores[position, :, across].reshape(chunk // 8, 8, SUB)
        weights = jnp.exp2((s - tops[:, across][None]) * LOG2E_SCALE).reshape(chunk, SUB).astype(BF16)
        sums[:, across] += jnp.dot(vt[position], weights, preferred_element_type=F32)

    def settle():
        tops[...] = jnp.broadcast_to(jnp.max(peaks[...], axis=0, keepdims=True), (8, tile))

    sub = lax.broadcasted_iota(jnp.int32, (16, 128), 0)
    blocks = tile // 128

    def finish(tile_index):
        for block in range(blocks):
            across = slice(block * 128, (block + 1) * 128)
            rows = sums[0:HD, across].T.astype(BF16)
            lines = jnp.zeros((16, 128), F32)
            if tile_index:
                lines = msg_ref[0, 2 * block, 64:80, :].astype(F32)
            values = split3(tops[0:1, across] * LOG2E_SCALE) + split3(sums[HD : HD + 1, across])
            for i, value in enumerate(values):
                lines = jnp.where(sub == 6 * tile_index + i, jnp.broadcast_to(value, (16, 128)), lines)
            msg_ref[0, 2 * block, 64:80, :] = lines.astype(BF16)
            turned = jnp.concatenate([lines[:, 64:128], lines[:, 0:64]], axis=1)
            msg_ref[0, 2 * block + 1, 64:80, :] = turned.astype(BF16)
            for part in range(2):
                msg_ref[tile_index, 2 * block + part, 0:64, :] = rows[part * 64 : (part + 1) * 64]

    def grouped(count, step):
        def turn(i):
            for k in range(GROUP):
                step(GROUP * i + k)

        loop(0, count // GROUP, turn)
        loop(count // GROUP * GROUP, count, step)

    def over_chunks(step):
        grouped(clear, lambda c: step(c, False))
        loop(clear, chunks, lambda c: step(c, True))

    def score_all(c, masked):
        turn_values(c)
        for part in range(parts):
            score(0, c, masked, part)

    peaks[...] = jnp.full_like(peaks, NEG)
    over_chunks(score_all)
    settle()

    for t in range(1, pieces):
        peaks[...] = jnp.full_like(peaks, NEG)
        sums[...] = jnp.zeros_like(sums)

        def both(c, masked, t=t):
            for part in range(parts):
                mix(c, part)
                score(t, c, masked, part)

        over_chunks(both)
        finish(t - 1)
        settle()

    def mix_all(c):
        for part in range(parts):
            mix(c, part)

    sums[...] = jnp.zeros_like(sums)
    grouped(chunks, mix_all)
    finish(pieces - 1)


def attend(queries, keys, values, keys_b, values_b, meta, start, layers, chunk):
    devices, rows, _ = queries.shape
    pages = meta.shape[0]
    slots = pages * PAGE
    heads = HEADS_HERE // 2
    pieces = 2
    piece = devices * rows // (heads * pieces)
    tile = heads * piece
    dma = pltpu.SemaphoreType.DMA
    vmem = pl.BlockSpec(memory_space=pltpu.VMEM)
    smem = pl.BlockSpec(memory_space=pltpu.SMEM)
    anywhere = pl.BlockSpec(memory_space=pl.ANY)
    return pl.pallas_call(
        functools.partial(attend_kernel, chunk, layers),
        out_shape=jax.ShapeDtypeStruct((pieces, devices // 2, 80, HD), BF16),
        in_specs=[smem, smem] + [anywhere] * 5,
        out_specs=vmem,
        scratch_shapes=[
            pltpu.VMEM(queries.shape, BF16),
            dma,
            pltpu.VMEM((pages, PAGE, HD), BF16),
            pltpu.VMEM((pages, PAGE, HD), BF16),
            dma((pages,)),
            dma((pages,)),
            pltpu.VMEM((slots + chunk, HD), BF16),
            pltpu.VMEM((slots + chunk, HD), F32),
            pltpu.VMEM((slots + chunk, HD), jnp.int32),
            pltpu.VMEM((slots // chunk, HD + 16, chunk), BF16),
            pltpu.VMEM((pieces, heads, piece, HD), BF16),
            pltpu.VMEM((slots // chunk, chunk, tile), F32),
            pltpu.VMEM((8, tile), F32),
            pltpu.VMEM((8, tile), F32),
            pltpu.VMEM((HD + 16, tile), F32),
            pltpu.VMEM((16, HD), BF16),
        ],
        compiler_params=pltpu.CompilerParams(vmem_limit_bytes=52 * 1024 * 1024),
        name="attend",
    )(meta, start, queries, keys, values, keys_b, values_b)


def split3(row):
    high = row.astype(BF16).astype(F32)
    rest = row - high
    middle = rest.astype(BF16).astype(F32)
    return high, middle, rest - middle


def finish_kernel(
    chips, layers, msg_ref, w_ref, att_ref, z_ref,
    w, in_msg, own_chunk, gathered, natural, terms,
    local_sems, a_send, a_recv, g_send, g_recv, s_send, s_recv, z_send, z_recv,
):
    ctx = lax.axis_index("ctx")
    layer = lax.axis_index("kvh")
    chip, core = ctx // 2, lax.rem(ctx, 2)
    other = {"ctx": ctx + 1 - 2 * core}
    tokens_here, heads, _ = att_ref.shape
    pieces = msg_ref.shape[0]
    _, per_layer, width = z_ref.shape
    half_heads = heads // 2
    depth = half_heads * HD
    piece = chips * 64 // half_heads

    def extent(s):
        return pl.ds(0, 64 if s else 80)

    load_w = pltpu.make_async_copy(w_ref, w, local_sems.at[pieces])
    load_own = [
        pltpu.make_async_copy(msg_ref.at[s, chip, extent(s)], in_msg.at[s, chip, extent(s)], local_sems.at[s])
        for s in range(pieces)
    ]
    peers = [partner(chip, chips, step) for step in steps(chips)]
    far_layers = sorted(range(1, layers), key=lambda k: -min(k, layers - k))
    greet_start(
        [{"ctx": peer * 2 + core} for peer in peers]
        + [{"kvh": lax.rem(layer + k, layers)} for k in far_layers]
        + [other]
    )
    for copy in load_own:
        copy.start()
    load_w.start()
    pl.semaphore_wait(pltpu.get_barrier_semaphore(), chips + layers - 1)

    for s in range(pieces):
        for peer in peers:
            remote(
                msg_ref.at[s, peer, extent(s)], in_msg.at[s, chip, extent(s)], a_send.at[s], a_recv.at[s],
                {"ctx": peer * 2 + core},
            ).start()
    pad = jnp.zeros((128 - chips, 128), F32)
    rest = pl.ds(0, chips - 1)

    def combine(s):
        load_own[s].wait()
        landed(in_msg.at[s, rest, extent(s)], a_recv.at[s])
        tops_in, totals_in = [], []
        for source in range(chips):
            lines = in_msg[0, source, 64:80, :].astype(F32)[6 * s : 6 * s + 6]
            tops_in.append(lines[0:1] + lines[1:2] + lines[2:3])
            totals_in.append(lines[3:4] + lines[4:5] + lines[5:6])
        top = jnp.concatenate(tops_in, axis=0)
        scale = jnp.exp2(top - jnp.max(top, axis=0, keepdims=True))
        total = jnp.sum(scale * jnp.concatenate(totals_in, axis=0), axis=0, keepdims=True)
        turned = jnp.concatenate([scale / total, pad], axis=0).T
        attention = jnp.zeros((64, HD), F32)
        for source in range(chips):
            attention = attention + turned[0:64, source : source + 1] * in_msg[s, source, 0:64, :].astype(F32)
        own_chunk[s] = attention.astype(BF16)
        gathered[s, core, chip] = own_chunk[s]

    def pair_copy(s):
        return remote(gathered.at[s, core], gathered.at[s, core], s_send.at[s], s_recv.at[s], other)

    def product(s, which):
        block = gathered[s, which].reshape(half_heads, piece, HD)
        columns = [block[head] for head in range(half_heads)]
        rows = pl.ds(pl.multiple_of(which * depth, depth), depth)
        return jnp.dot(jnp.concatenate(columns, axis=1), w[rows, :], preferred_element_type=F32)

    for s in range(pieces):
        combine(s)
        for peer in peers:
            remote(
                own_chunk.at[s], gathered.at[s, core, chip], g_send.at[s], g_recv.at[s], {"ctx": peer * 2 + core}
            ).start()
    load_w.wait()
    for s in range(pieces):
        landed(gathered.at[s, core, rest], g_recv.at[s])
        pair_copy(s).start()
        held = product(s, core)
        landed(gathered.at[s, 1 - core], s_recv.at[s])
        ready = (held + product(s, 1 - core)).astype(BF16).reshape(layers // pieces, per_layer, width)
        for j in range(layers // pieces):
            terms[pieces * j + s] = ready[j]
        nearest = layer + lax.rem(layer + s, pieces)
        for k in sorted(range(0, layers, pieces), key=lambda k: -min(k, layers - k)):
            target = lax.rem(nearest + k, layers)

            @pl.when(layer != target)
            def _(target=target):
                remote(terms.at[target], z_ref.at[layer], z_send, z_recv, {"kvh": target}).start()

    keep = pltpu.make_async_copy(terms.at[layer], z_ref.at[layer], local_sems.at[0])
    keep.start()

    two = 2 * tokens_here
    block = chip * two // per_layer
    line = block // pieces * per_layer + lax.rem(chip * two, per_layer)
    for head in range(heads):
        flat = head % half_heads * piece + line
        rows = pl.ds(pl.multiple_of(lax.rem(flat, 64), two), two)
        both = gathered[lax.rem(block, pieces), head // half_heads, flat // 64, rows, :].astype(F32)
        mine = jnp.where(core == 0, both[0:tokens_here], both[tokens_here:two])
        natural[pl.ds(head, tokens_here, stride=heads), :] = mine
    att_ref[...] = natural[...].astype(BF16).reshape(att_ref.shape)

    for s in range(pieces):
        landed(in_msg.at[s, rest, extent(s)], a_send.at[s])
        landed(gathered.at[s, core, rest], g_send.at[s])
        pair_copy(s).wait_send()
    keep.wait()
    layers_rest = z_ref.at[pl.ds(0, layers - 1)]
    landed(layers_rest, z_send)
    landed(layers_rest, z_recv)


def finish(mesh, messages, out_weight, tokens_here):
    chips, layers = mesh.shape["ctx"] // 2, mesh.shape["kvh"]
    width = out_weight.shape[1]
    tokens = chips * 2 * tokens_here
    dma = pltpu.SemaphoreType.DMA
    vmem = pl.BlockSpec(memory_space=pltpu.VMEM)
    anywhere = pl.BlockSpec(memory_space=pl.ANY)
    pieces = messages.shape[0]
    return pl.pallas_call(
        functools.partial(finish_kernel, chips, layers),
        out_shape=(
            jax.ShapeDtypeStruct((tokens_here, HEADS_HERE, HD), BF16),
            jax.ShapeDtypeStruct((layers, tokens // layers, width), BF16),
        ),
        in_specs=[anywhere] * 2,
        out_specs=(vmem, anywhere),
        scratch_shapes=[
            pltpu.VMEM(out_weight.shape, BF16),
            pltpu.VMEM(messages.shape, BF16),
            pltpu.VMEM((pieces, 64, HD), BF16),
            pltpu.VMEM((pieces, 2, chips, 64, HD), BF16),
            pltpu.VMEM((HEADS_HERE * tokens_here, HD), F32),
            pltpu.VMEM((layers, tokens // layers, width), BF16),
            dma((pieces + 1,)),
            dma((pieces,)),
            dma((pieces,)),
            dma((pieces,)),
            dma((pieces,)),
            dma((pieces,)),
            dma((pieces,)),
            dma,
            dma,
        ],
        compiler_params=pltpu.CompilerParams(
            collective_id=1, has_side_effects=True, vmem_limit_bytes=24 * 1024 * 1024
        ),
        name="finish",
    )(messages, out_weight)


def total_kernel(att_ref, z_ref, att_out, proj_out):
    att_out[...] = att_ref[...]
    projected = z_ref[0].astype(F32)
    for source in range(1, z_ref.shape[0]):
        projected = projected + z_ref[source].astype(F32)
    proj_out[...] = projected.astype(BF16)


def total(attention, terms):
    vmem = pl.BlockSpec(memory_space=pltpu.VMEM)
    return pl.pallas_call(
        total_kernel,
        out_shape=(
            jax.ShapeDtypeStruct(attention.shape, BF16),
            jax.ShapeDtypeStruct(terms.shape[1:], BF16),
        ),
        in_specs=[vmem] * 2,
        out_specs=(vmem, vmem),
        compiler_params=pltpu.CompilerParams(vmem_limit_bytes=24 * 1024 * 1024),
        name="total",
    )(attention, terms)


def solution(mesh, chunk=512):
    def local(queries, key_cache, value_cache, block_lengths, block_home, stretch_start, out_weight):
        slots = key_cache.shape[0]
        keys, values = key_cache.reshape(slots, HD), value_cache.reshape(slots, HD)
        qall, keys_b, values_b, meta = gather_queries(mesh, queries, block_lengths, block_home, keys, values)
        messages = attend(qall, keys, values, keys_b, values_b, meta, stretch_start, mesh.shape["kvh"], chunk)
        return total(*finish(mesh, messages, out_weight, queries.shape[0]))

    in_specs = (
        P("ctx", "kvh", None),
        P("ctx", "kvh", None),
        P("ctx", "kvh", None),
        P(),
        P(),
        P(),
        P("kvh", "ctx"),
    )
    out_specs = (P("ctx", "kvh", None), P("kvh", "ctx"))
    return jax.shard_map(local, mesh=mesh, in_specs=in_specs, out_specs=out_specs, check_vma=False)
```

```python
import functools
import math

import jax
import jax.numpy as jnp
from jax import lax
from jax.experimental import pallas as pl
from jax.experimental.pallas import tpu as pltpu
from jax.sharding import PartitionSpec as P

HD = 128
PAGE = 256
HEADS_HERE = 16
SUB = 256
GROUP = 3
NEG = -1e30
FAR = 1 << 30
LOG2E_SCALE = math.log2(math.e) / math.sqrt(HD)
F32 = jnp.float32
BF16 = jnp.bfloat16
VMEM_LIMIT = 56 * 1024 * 1024


def greet_start(devices):
    for device in devices:
        pl.semaphore_signal(
            pltpu.get_barrier_semaphore(), inc=1, device_id=device, device_id_type=pl.DeviceIdType.MESH
        )


def remote(src, dst, send, recv, device):
    return pltpu.make_async_remote_copy(
        src_ref=src,
        dst_ref=dst,
        send_sem=send,
        recv_sem=recv,
        device_id=device,
        device_id_type=pl.DeviceIdType.MESH,
    )


def loop(start, stop, body):
    def step(k, _):
        body(k)
        return 0

    lax.fori_loop(start, stop, step, 0)


def partner(chip, chips, step):
    if chips != 16:
        return lax.rem(chip + step, chips)
    return lax.rem(chip // 4 + step // 4, 4) * 4 + lax.rem(chip + step, 4)


def steps(chips):
    if chips != 16:
        return list(range(1, chips))
    near = [0, 1, 2, 1]
    return sorted(range(1, chips), key=lambda step: -(near[step // 4] + near[step % 4]))


def landed(buffer, sem):
    pltpu.make_async_copy(buffer, buffer, sem).wait()


def gather_kernel(
    devices, q_ref, len_ref, home_ref, k_ref, v_ref, all_ref, meta_ref,
    q_in, len_in, home_in, mine, natural, send, recv, kv_send, kv_recv, own_sem, in_sems,
):
    ctx = lax.axis_index("ctx")
    core = lax.rem(ctx, 2)
    other = {"ctx": ctx + 1 - 2 * core}
    tokens, heads = q_ref.shape[0], q_ref.shape[1]
    half = heads // 2
    blocks_here = k_ref.shape[0]
    first_q = 2 * blocks_here
    loads = [
        pltpu.make_async_copy(source, target, in_sems.at[i])
        for i, (source, target) in enumerate([(q_ref, q_in), (len_ref, len_in), (home_ref, home_in)])
    ]
    for load in loads:
        load.start()
    chip, chips = ctx // 2, devices // 2
    peers = [partner(chip, chips, step) * 2 + side for step in steps(chips) for side in range(2)]
    peers.append(ctx + 1 - 2 * core)
    greet_start([{"ctx": peer} for peer in peers])
    loads[0].wait()
    natural[...] = q_in[...].astype(F32).reshape(tokens * heads, HD)
    for part in range(2):
        rows = [natural[pl.ds(part * half + head, tokens, stride=heads), :] for head in range(half)]
        mine[part] = jnp.concatenate(rows, axis=0).astype(BF16)
    pl.semaphore_wait(pltpu.get_barrier_semaphore(), devices - 1)

    for peer in peers:
        remote(mine.at[lax.rem(peer, 2)], all_ref.at[first_q + ctx], send, recv, {"ctx": peer}).start()
    own = pltpu.make_async_copy(mine.at[core], all_ref.at[first_q + ctx], own_sem)
    own.start()
    pairs = [
        remote(k_ref, all_ref.at[pl.ds(0, blocks_here)], kv_send.at[0], kv_recv.at[0], other),
        remote(v_ref, all_ref.at[pl.ds(blocks_here, blocks_here)], kv_send.at[1], kv_recv.at[1], other),
    ]
    for pair in pairs:
        pair.start()

    pages, blocks = meta_ref.shape[0], home_ref.shape[1]
    loads[1].wait()
    loads[2].wait()
    lengths = len_in[...].astype(F32)
    index = lax.broadcasted_iota(jnp.int32, (pages, blocks), 0)
    here = pages // 2
    stored = jnp.where(index < here, ctx * here + index, (ctx + 1 - 2 * core) * here + index - here)
    logical = lax.broadcasted_iota(jnp.int32, (pages, blocks), 1).astype(F32)
    match = home_in[...] == stored
    place = jnp.sum(jnp.where(match, logical, 0.0), axis=1, keepdims=True)
    filled = jnp.sum(jnp.where(match, lengths, 0.0), axis=1, keepdims=True)
    begin = jnp.sum(jnp.where(logical < place, lengths, 0.0), axis=1, keepdims=True)
    lane = lax.broadcasted_iota(jnp.int32, (pages, 128), 1)
    meta = jnp.where(lane == 0, begin, jnp.where(lane == 1, filled, 0.0))
    meta_ref[...] = meta.astype(jnp.int32)

    own.wait()

    others = all_ref.at[pl.ds(first_q, devices - 1)]
    landed(others, recv)
    for pair in pairs:
        pair.wait()
    landed(others, send)


def gather_queries(mesh, queries, block_lengths, block_home, keys, values):
    devices = mesh.shape["ctx"]
    tokens, heads, _ = queries.shape
    rows = tokens * heads // 2
    pages = 2 * keys.shape[0] * rows // PAGE
    dma = pltpu.SemaphoreType.DMA
    vmem = pl.BlockSpec(memory_space=pltpu.VMEM)
    anywhere = pl.BlockSpec(memory_space=pl.ANY)
    return pl.pallas_call(
        functools.partial(gather_kernel, devices),
        out_shape=(
            jax.ShapeDtypeStruct((2 * keys.shape[0] + devices, rows, HD), BF16),
            jax.ShapeDtypeStruct((pages, 128), jnp.int32),
        ),
        in_specs=[anywhere] * 5,
        out_specs=(anywhere, vmem),
        scratch_shapes=[
            pltpu.VMEM(queries.shape, BF16),
            pltpu.VMEM((1, block_lengths.shape[0]), jnp.int32),
            pltpu.VMEM((1, block_home.shape[0]), jnp.int32),
            pltpu.VMEM((2, rows, HD), BF16),
            pltpu.VMEM((2 * rows, HD), F32),
            dma,
            dma,
            dma((2,)),
            dma((2,)),
            dma,
            dma((3,)),
        ],
        compiler_params=pltpu.CompilerParams(
            collective_id=0, has_side_effects=True, vmem_limit_bytes=VMEM_LIMIT
        ),
        name="gather_queries",
    )(queries, block_lengths.reshape(1, -1), block_home.reshape(1, -1), keys, values)


def attend_kernel(
    chunk, layers,
    meta_ref, start_ref, k_a, v_a, other_ref, msg_ref,
    q_in, q_sem, k_in, v_in, k_sem, v_sem, kc, vc, where_at, vt, qh, scores, peaks, tops, sums, tail,
):
    pages = meta_ref.shape[0]
    pieces, heads, piece, _ = qh.shape
    devices = q_in.shape[0]
    tile = heads * piece
    tokens = pieces * piece
    tokens_here = tokens // devices
    two = 2 * tokens_here
    per_layer = tokens // layers
    first = start_ref[0]
    last = first + tokens - 1
    slot = lax.broadcasted_iota(jnp.int32, (PAGE, HD), 0)
    here = pages // 2

    def fetch(page, keys, values):
        source = pl.ds(lax.rem(page, here) * k_in.shape[1], k_in.shape[1])
        return (
            pltpu.make_async_copy(keys.at[source], k_in.at[page], k_sem.at[page]),
            pltpu.make_async_copy(values.at[source], v_in.at[page], v_sem.at[page]),
        )

    def request(page, keys, values):
        @pl.when(meta_ref[page, 0] <= last)
        def _():
            for copy in fetch(page, keys, values):
                copy.start()

    count = k_a.shape[0]
    k_b, v_b = other_ref.at[pl.ds(0, count)], other_ref.at[pl.ds(count, count)]
    load_q = pltpu.make_async_copy(other_ref.at[pl.ds(2 * count, devices)], q_in, q_sem)
    load_q.start()
    loop(0, here, lambda p: request(p, k_a, v_a))
    loop(here, pages, lambda p: request(p, k_b, v_b))

    def arrange(chip):
        block = q_in[pl.ds(2 * chip, 2)].astype(F32).reshape(2, heads, tokens_here, HD)
        layer = chip * two // per_layer
        line = layer // pieces * per_layer + lax.rem(chip * two, per_layer)
        target = pl.ds(pl.multiple_of(line, two), two)
        for head in range(heads):
            rows = jnp.concatenate([block[0, head], block[1, head]], axis=0)
            qh[lax.rem(layer, pieces), head, target, :] = rows.astype(BF16)

    def visit(page, used, masked):
        begin, filled = meta_ref[page, 0], meta_ref[page, 1]
        partly = begin + filled - 1 > first
        seen = begin <= last
        take = jnp.logical_and(seen, partly) if masked else jnp.logical_not(partly)

        @pl.when(take)
        def _():
            target = pl.ds(pl.multiple_of(used, 16), PAGE)
            for copy in fetch(page, k_a, v_a):
                copy.wait()
            keys = k_in[page].reshape(PAGE, HD).astype(F32)
            live = slot < filled
            lead = jnp.broadcast_to(keys[0:1, :], (PAGE, HD))
            kc[target, :] = jnp.where(live, keys, lead).astype(BF16)
            tail[...] = lead[0:16, :].astype(BF16)
            vc[target, :] = jnp.where(live, v_in[page].reshape(PAGE, HD).astype(F32), 0.0)
            where_at[target, :] = jnp.where(live, begin + slot, FAR)

        return used + jnp.where(take, (filled + 15) // 16 * 16, 0)

    tail[...] = jnp.zeros_like(tail)
    plain = lax.fori_loop(0, pages, lambda p, u: visit(p, u, False), jnp.int32(0))
    used = lax.fori_loop(0, pages, lambda p, u: visit(p, u, True), plain)
    ending = pl.ds(pl.multiple_of(used, 16), chunk)
    kc[ending, :] = jnp.concatenate([tail[...]] * (chunk // 16), axis=0)
    vc[ending, :] = jnp.zeros((chunk, HD), F32)
    where_at[ending, :] = jnp.full((chunk, HD), FAR, jnp.int32)
    load_q.wait()
    loop(0, devices // 2, arrange)
    chunks = (used + chunk - 1) // chunk
    clear = jnp.where(used > plain, plain // chunk, chunks)
    per_part = SUB // piece
    parts = tile // SUB
    line = lax.broadcasted_iota(jnp.int32, (1, piece), 1)

    def span(position):
        return pl.ds(pl.multiple_of(position * chunk, chunk), chunk)

    def turn_values(position):
        vt[position, 0:HD, :] = vc[span(position), :].T.astype(BF16)
        live = jnp.where(where_at[span(position), :] < FAR, 1.0, 0.0).T
        vt[position, HD : HD + 16, :] = live[0:16, :].astype(BF16)

    def score(tile_index, position, masked, part):
        q = qh[tile_index, part * per_part : (part + 1) * per_part].reshape(SUB, HD)
        s = lax.dot_general(kc[span(position), :], q, (((1,), (1,)), ((), ())), preferred_element_type=F32)
        if masked:
            token = (line // per_layer * pieces + tile_index) * per_layer + lax.rem(line, per_layer)
            seen = where_at[span(position), 0:piece] <= first + token
            s = jnp.concatenate(
                [jnp.where(seen, s[:, head * piece : (head + 1) * piece], NEG) for head in range(per_part)], axis=1
            )
        across = slice(part * SUB, (part + 1) * SUB)
        scores[position, :, across] = s
        peaks[:, across] = jnp.maximum(peaks[:, across], jnp.max(s.reshape(chunk // 8, 8, SUB), axis=0))

    def mix(position, part):
        across = slice(part * SUB, (part + 1) * SUB)
        s = scores[position, :, across].reshape(chunk // 8, 8, SUB)
        weights = jnp.exp2((s - tops[:, across][None]) * LOG2E_SCALE).reshape(chunk, SUB).astype(BF16)
        sums[:, across] += jnp.dot(vt[position], weights, preferred_element_type=F32)

    def settle():
        tops[...] = jnp.broadcast_to(jnp.max(peaks[...], axis=0, keepdims=True), (8, tile))

    sub = lax.broadcasted_iota(jnp.int32, (16, 128), 0)
    blocks = tile // 128

    def finish(tile_index):
        for block in range(blocks):
            across = slice(block * 128, (block + 1) * 128)
            rows = sums[0:HD, across].T.astype(BF16)
            lines = jnp.zeros((16, 128), F32)
            if tile_index:
                lines = msg_ref[0, 2 * block, 64:80, :].astype(F32)
            values = split3(tops[0:1, across] * LOG2E_SCALE) + split3(sums[HD : HD + 1, across])
            for i, value in enumerate(values):
                lines = jnp.where(sub == 6 * tile_index + i, jnp.broadcast_to(value, (16, 128)), lines)
            msg_ref[0, 2 * block, 64:80, :] = lines.astype(BF16)
            turned = jnp.concatenate([lines[:, 64:128], lines[:, 0:64]], axis=1)
            msg_ref[0, 2 * block + 1, 64:80, :] = turned.astype(BF16)
            for part in range(2):
                msg_ref[tile_index, 2 * block + part, 0:64, :] = rows[part * 64 : (part + 1) * 64]

    def grouped(count, step):
        def turn(i):
            for k in range(GROUP):
                step(GROUP * i + k)

        loop(0, count // GROUP, turn)
        loop(count // GROUP * GROUP, count, step)

    def over_chunks(step):
        grouped(clear, lambda c: step(c, False))
        loop(clear, chunks, lambda c: step(c, True))

    def score_all(c, masked):
        turn_values(c)
        for part in range(parts):
            score(0, c, masked, part)

    peaks[...] = jnp.full_like(peaks, NEG)
    over_chunks(score_all)
    settle()

    for t in range(1, pieces):
        peaks[...] = jnp.full_like(peaks, NEG)
        sums[...] = jnp.zeros_like(sums)

        def both(c, masked, t=t):
            for part in range(parts):
                mix(c, part)
                score(t, c, masked, part)

        over_chunks(both)
        finish(t - 1)
        settle()

    def mix_all(c):
        for part in range(parts):
            mix(c, part)

    sums[...] = jnp.zeros_like(sums)
    grouped(chunks, mix_all)
    finish(pieces - 1)


def attend(keys, values, others, meta, start, layers, chunk):
    rows = others.shape[1]
    devices = others.shape[0] - 2 * keys.shape[0]
    pages = meta.shape[0]
    slots = pages * PAGE
    heads = HEADS_HERE // 2
    pieces = 2
    piece = devices * rows // (heads * pieces)
    tile = heads * piece
    dma = pltpu.SemaphoreType.DMA
    vmem = pl.BlockSpec(memory_space=pltpu.VMEM)
    smem = pl.BlockSpec(memory_space=pltpu.SMEM)
    anywhere = pl.BlockSpec(memory_space=pl.ANY)
    return pl.pallas_call(
        functools.partial(attend_kernel, chunk, layers),
        out_shape=jax.ShapeDtypeStruct((pieces, devices // 2, 80, HD), BF16),
        in_specs=[smem, smem] + [anywhere] * 3,
        out_specs=vmem,
        scratch_shapes=[
            pltpu.VMEM((devices, rows, HD), BF16),
            dma,
            pltpu.VMEM((pages, PAGE // rows, rows, HD), BF16),
            pltpu.VMEM((pages, PAGE // rows, rows, HD), BF16),
            dma((pages,)),
            dma((pages,)),
            pltpu.VMEM((slots + chunk, HD), BF16),
            pltpu.VMEM((slots + chunk, HD), F32),
            pltpu.VMEM((slots + chunk, HD), jnp.int32),
            pltpu.VMEM((slots // chunk, HD + 16, chunk), BF16),
            pltpu.VMEM((pieces, heads, piece, HD), BF16),
            pltpu.VMEM((slots // chunk, chunk, tile), F32),
            pltpu.VMEM((8, tile), F32),
            pltpu.VMEM((8, tile), F32),
            pltpu.VMEM((HD + 16, tile), F32),
            pltpu.VMEM((16, HD), BF16),
        ],
        compiler_params=pltpu.CompilerParams(vmem_limit_bytes=52 * 1024 * 1024),
        name="attend",
    )(meta, start, keys, values, others)


def split3(row):
    high = row.astype(BF16).astype(F32)
    rest = row - high
    middle = rest.astype(BF16).astype(F32)
    return high, middle, rest - middle


def finish_kernel(
    chips, layers, msg_ref, w_ref, att_ref, z_ref,
    w, in_msg, own_chunk, gathered, natural, terms,
    local_sems, a_send, a_recv, g_send, g_recv, s_send, s_recv, z_send, z_recv,
):
    ctx = lax.axis_index("ctx")
    layer = lax.axis_index("kvh")
    chip, core = ctx // 2, lax.rem(ctx, 2)
    other = {"ctx": ctx + 1 - 2 * core}
    tokens_here, heads, _ = att_ref.shape
    pieces = msg_ref.shape[0]
    _, per_layer, width = z_ref.shape
    half_heads = heads // 2
    depth = half_heads * HD
    piece = chips * 64 // half_heads

    def extent(s):
        return pl.ds(0, 64 if s else 80)

    load_w = pltpu.make_async_copy(w_ref, w, local_sems.at[pieces])
    load_own = [
        pltpu.make_async_copy(msg_ref.at[s, chip, extent(s)], in_msg.at[s, chip, extent(s)], local_sems.at[s])
        for s in range(pieces)
    ]
    peers = [partner(chip, chips, step) for step in steps(chips)]
    far_layers = sorted(range(1, layers), key=lambda k: -min(k, layers - k))
    greet_start(
        [{"ctx": peer * 2 + core} for peer in peers]
        + [{"kvh": lax.rem(layer + k, layers)} for k in far_layers]
        + [other]
    )
    for copy in load_own:
        copy.start()
    load_w.start()
    pl.semaphore_wait(pltpu.get_barrier_semaphore(), chips + layers - 1)

    for s in range(pieces):
        for peer in peers:
            remote(
                msg_ref.at[s, peer, extent(s)], in_msg.at[s, chip, extent(s)], a_send.at[s], a_recv.at[s],
                {"ctx": peer * 2 + core},
            ).start()
    pad = jnp.zeros((128 - chips, 128), F32)
    rest = pl.ds(0, chips - 1)

    def combine(s):
        load_own[s].wait()
        landed(in_msg.at[s, rest, extent(s)], a_recv.at[s])
        tops_in, totals_in = [], []
        for source in range(chips):
            lines = in_msg[0, source, 64:80, :].astype(F32)[6 * s : 6 * s + 6]
            tops_in.append(lines[0:1] + lines[1:2] + lines[2:3])
            totals_in.append(lines[3:4] + lines[4:5] + lines[5:6])
        top = jnp.concatenate(tops_in, axis=0)
        scale = jnp.exp2(top - jnp.max(top, axis=0, keepdims=True))
        total = jnp.sum(scale * jnp.concatenate(totals_in, axis=0), axis=0, keepdims=True)
        turned = jnp.concatenate([scale / total, pad], axis=0).T
        attention = jnp.zeros((64, HD), F32)
        for source in range(chips):
            attention = attention + turned[0:64, source : source + 1] * in_msg[s, source, 0:64, :].astype(F32)
        own_chunk[s] = attention.astype(BF16)
        gathered[s, core, chip] = own_chunk[s]

    def pair_copy(s):
        return remote(gathered.at[s, core], gathered.at[s, core], s_send.at[s], s_recv.at[s], other)

    def product(s, which):
        block = gathered[s, which].reshape(half_heads, piece, HD)
        columns = [block[head] for head in range(half_heads)]
        rows = pl.ds(pl.multiple_of(which * depth, depth), depth)
        return jnp.dot(jnp.concatenate(columns, axis=1), w[rows, :], preferred_element_type=F32)

    for s in range(pieces):
        combine(s)
        for peer in peers:
            remote(
                own_chunk.at[s], gathered.at[s, core, chip], g_send.at[s], g_recv.at[s], {"ctx": peer * 2 + core}
            ).start()
    load_w.wait()
    for s in range(pieces):
        landed(gathered.at[s, core, rest], g_recv.at[s])
        pair_copy(s).start()
        held = product(s, core)
        landed(gathered.at[s, 1 - core], s_recv.at[s])
        ready = (held + product(s, 1 - core)).astype(BF16).reshape(layers // pieces, per_layer, width)
        for j in range(layers // pieces):
            terms[pieces * j + s] = ready[j]
        nearest = layer + lax.rem(layer + s, pieces)
        for k in sorted(range(0, layers, pieces), key=lambda k: -min(k, layers - k)):
            target = lax.rem(nearest + k, layers)

            @pl.when(layer != target)
            def _(target=target):
                remote(terms.at[target], z_ref.at[layer], z_send, z_recv, {"kvh": target}).start()

    keep = pltpu.make_async_copy(terms.at[layer], z_ref.at[layer], local_sems.at[0])
    keep.start()

    two = 2 * tokens_here
    block = chip * two // per_layer
    line = block // pieces * per_layer + lax.rem(chip * two, per_layer)
    for head in range(heads):
        flat = head % half_heads * piece + line
        rows = pl.ds(pl.multiple_of(lax.rem(flat, 64), two), two)
        both = gathered[lax.rem(block, pieces), head // half_heads, flat // 64, rows, :].astype(F32)
        mine = jnp.where(core == 0, both[0:tokens_here], both[tokens_here:two])
        natural[pl.ds(head, tokens_here, stride=heads), :] = mine
    att_ref[...] = natural[...].astype(BF16).reshape(att_ref.shape)

    for s in range(pieces):
        landed(in_msg.at[s, rest, extent(s)], a_send.at[s])
        landed(gathered.at[s, core, rest], g_send.at[s])
        pair_copy(s).wait_send()
    keep.wait()
    layers_rest = z_ref.at[pl.ds(0, layers - 1)]
    landed(layers_rest, z_send)
    landed(layers_rest, z_recv)


def finish(mesh, messages, out_weight, tokens_here):
    chips, layers = mesh.shape["ctx"] // 2, mesh.shape["kvh"]
    width = out_weight.shape[1]
    tokens = chips * 2 * tokens_here
    dma = pltpu.SemaphoreType.DMA
    vmem = pl.BlockSpec(memory_space=pltpu.VMEM)
    anywhere = pl.BlockSpec(memory_space=pl.ANY)
    pieces = messages.shape[0]
    return pl.pallas_call(
        functools.partial(finish_kernel, chips, layers),
        out_shape=(
            jax.ShapeDtypeStruct((tokens_here, HEADS_HERE, HD), BF16),
            jax.ShapeDtypeStruct((layers, tokens // layers, width), BF16),
        ),
        in_specs=[anywhere] * 2,
        out_specs=(vmem, anywhere),
        scratch_shapes=[
            pltpu.VMEM(out_weight.shape, BF16),
            pltpu.VMEM(messages.shape, BF16),
            pltpu.VMEM((pieces, 64, HD), BF16),
            pltpu.VMEM((pieces, 2, chips, 64, HD), BF16),
            pltpu.VMEM((HEADS_HERE * tokens_here, HD), F32),
            pltpu.VMEM((layers, tokens // layers, width), BF16),
            dma((pieces + 1,)),
            dma((pieces,)),
            dma((pieces,)),
            dma((pieces,)),
            dma((pieces,)),
            dma((pieces,)),
            dma((pieces,)),
            dma,
            dma,
        ],
        compiler_params=pltpu.CompilerParams(
            collective_id=1, has_side_effects=True, vmem_limit_bytes=24 * 1024 * 1024
        ),
        name="finish",
    )(messages, out_weight)


def total_kernel(att_ref, z_ref, att_out, proj_out):
    att_out[...] = att_ref[...]
    projected = z_ref[0].astype(F32)
    for source in range(1, z_ref.shape[0]):
        projected = projected + z_ref[source].astype(F32)
    proj_out[...] = projected.astype(BF16)


def total(attention, terms):
    vmem = pl.BlockSpec(memory_space=pltpu.VMEM)
    return pl.pallas_call(
        total_kernel,
        out_shape=(
            jax.ShapeDtypeStruct(attention.shape, BF16),
            jax.ShapeDtypeStruct(terms.shape[1:], BF16),
        ),
        in_specs=[vmem] * 2,
        out_specs=(vmem, vmem),
        compiler_params=pltpu.CompilerParams(vmem_limit_bytes=24 * 1024 * 1024),
        name="total",
    )(attention, terms)


def solution(mesh, chunk=512):
    def local(queries, key_cache, value_cache, block_lengths, block_home, stretch_start, out_weight):
        rows = queries.shape[0] * queries.shape[1] // 2
        keys, values = key_cache.reshape(-1, rows, HD), value_cache.reshape(-1, rows, HD)
        others, meta = gather_queries(mesh, queries, block_lengths, block_home, keys, values)
        messages = attend(keys, values, others, meta, stretch_start, mesh.shape["kvh"], chunk)
        return total(*finish(mesh, messages, out_weight, queries.shape[0]))

    in_specs = (
        P("ctx", "kvh", None),
        P("ctx", "kvh", None),
        P("ctx", "kvh", None),
        P(),
        P(),
        P(),
        P("kvh", "ctx"),
    )
    out_specs = (P("ctx", "kvh", None), P("kvh", "ctx"))
    return jax.shard_map(local, mesh=mesh, in_specs=in_specs, out_specs=out_specs, check_vma=False)
```

```python
import functools
import math

import jax
import jax.numpy as jnp
from jax import lax
from jax.experimental import pallas as pl
from jax.experimental.pallas import tpu as pltpu
from jax.sharding import PartitionSpec as P

HD = 128
PAGE = 256
HEADS_HERE = 16
SUB = 256
GROUP = 3
NEG = -1e30
FAR = 1 << 30
META_ROWS = 8192
LOG2E_SCALE = math.log2(math.e) / math.sqrt(HD)
F32 = jnp.float32
BF16 = jnp.bfloat16
VMEM_LIMIT = 56 * 1024 * 1024


def greet_start(devices):
    for device in devices:
        pl.semaphore_signal(
            pltpu.get_barrier_semaphore(), inc=1, device_id=device, device_id_type=pl.DeviceIdType.MESH
        )


def remote(src, dst, send, recv, device):
    return pltpu.make_async_remote_copy(
        src_ref=src,
        dst_ref=dst,
        send_sem=send,
        recv_sem=recv,
        device_id=device,
        device_id_type=pl.DeviceIdType.MESH,
    )


def loop(start, stop, body):
    def step(k, _):
        body(k)
        return 0

    lax.fori_loop(start, stop, step, 0)


def partner(chip, chips, step):
    if chips != 16:
        return lax.rem(chip + step, chips)
    return lax.rem(chip // 4 + step // 4, 4) * 4 + lax.rem(chip + step, 4)


def steps(chips):
    if chips != 16:
        return list(range(1, chips))
    near = [0, 1, 2, 1]
    return sorted(range(1, chips), key=lambda step: -(near[step // 4] + near[step % 4]))


def landed(buffer, sem):
    pltpu.make_async_copy(buffer, buffer, sem).wait()


def gather_kernel(
    devices, q_ref, len_ref, home_ref, k_ref, v_ref, all_ref, meta_ref,
    q_in, len_in, home_in, facts, mine, natural, send, recv, kv_send, kv_recv, own_sem, in_sems,
):
    ctx = lax.axis_index("ctx")
    core = lax.rem(ctx, 2)
    other = {"ctx": ctx + 1 - 2 * core}
    tokens, heads = q_ref.shape[0], q_ref.shape[1]
    half = heads // 2
    blocks_here = k_ref.shape[0]
    first_q = 2 * blocks_here
    loads = [
        pltpu.make_async_copy(source, target, in_sems.at[i])
        for i, (source, target) in enumerate([(q_ref, q_in), (len_ref, len_in), (home_ref, home_in)])
    ]
    for load in loads:
        load.start()
    chip, chips = ctx // 2, devices // 2
    peers = [partner(chip, chips, step) * 2 + side for step in steps(chips) for side in range(2)]
    peers.append(ctx + 1 - 2 * core)
    greet_start([{"ctx": peer} for peer in peers])
    loads[0].wait()
    natural[...] = q_in[...].astype(F32).reshape(tokens * heads, HD)
    for part in range(2):
        rows = [natural[pl.ds(part * half + head, tokens, stride=heads), :] for head in range(half)]
        mine[part] = jnp.concatenate(rows, axis=0).astype(BF16)
    pl.semaphore_wait(pltpu.get_barrier_semaphore(), devices - 1)

    for peer in peers:
        remote(mine.at[lax.rem(peer, 2)], all_ref.at[first_q + ctx], send, recv, {"ctx": peer}).start()
    own = pltpu.make_async_copy(mine.at[core], all_ref.at[first_q + ctx], own_sem)
    own.start()
    pairs = [
        remote(k_ref, all_ref.at[pl.ds(0, blocks_here)], kv_send.at[0], kv_recv.at[0], other),
        remote(v_ref, all_ref.at[pl.ds(blocks_here, blocks_here)], kv_send.at[1], kv_recv.at[1], other),
    ]
    for pair in pairs:
        pair.start()

    pages, blocks = facts.shape[0], home_ref.shape[1]
    loads[1].wait()
    loads[2].wait()
    lengths = len_in[...].astype(F32)
    index = lax.broadcasted_iota(jnp.int32, (pages, blocks), 0)
    here = pages // 2
    stored = jnp.where(index < here, ctx * here + index, (ctx + 1 - 2 * core) * here + index - here)
    logical = lax.broadcasted_iota(jnp.int32, (pages, blocks), 1).astype(F32)
    match = home_in[...] == stored
    place = jnp.sum(jnp.where(match, logical, 0.0), axis=1, keepdims=True)
    filled = jnp.sum(jnp.where(match, lengths, 0.0), axis=1, keepdims=True)
    begin = jnp.sum(jnp.where(logical < place, lengths, 0.0), axis=1, keepdims=True)
    lane = lax.broadcasted_iota(jnp.int32, (pages, 128), 1)
    meta = jnp.where(lane == 0, begin, jnp.where(lane == 1, filled, 0.0))
    facts[...] = meta.astype(jnp.int32)
    publish = pltpu.make_async_copy(facts, meta_ref.at[pl.ds(0, pages)], in_sems.at[3])
    publish.start()

    own.wait()
    publish.wait()

    others = all_ref.at[pl.ds(first_q, devices - 1)]
    landed(others, recv)
    for pair in pairs:
        pair.wait()
    landed(others, send)


def gather_queries(mesh, queries, block_lengths, block_home, keys, values):
    devices = mesh.shape["ctx"]
    tokens, heads, _ = queries.shape
    rows = tokens * heads // 2
    pages = 2 * keys.shape[0] * rows // PAGE
    dma = pltpu.SemaphoreType.DMA
    anywhere = pl.BlockSpec(memory_space=pl.ANY)
    return pl.pallas_call(
        functools.partial(gather_kernel, devices),
        out_shape=(
            jax.ShapeDtypeStruct((2 * keys.shape[0] + devices, rows, HD), BF16),
            jax.ShapeDtypeStruct((META_ROWS, 128), jnp.int32),
        ),
        in_specs=[anywhere] * 5,
        out_specs=(anywhere, anywhere),
        scratch_shapes=[
            pltpu.VMEM(queries.shape, BF16),
            pltpu.VMEM((1, block_lengths.shape[0]), jnp.int32),
            pltpu.VMEM((1, block_home.shape[0]), jnp.int32),
            pltpu.VMEM((pages, 128), jnp.int32),
            pltpu.VMEM((2, rows, HD), BF16),
            pltpu.VMEM((2 * rows, HD), F32),
            dma,
            dma,
            dma((2,)),
            dma((2,)),
            dma,
            dma((4,)),
        ],
        compiler_params=pltpu.CompilerParams(
            collective_id=0, has_side_effects=True, vmem_limit_bytes=VMEM_LIMIT
        ),
        name="gather_queries",
    )(queries, block_lengths.reshape(1, -1), block_home.reshape(1, -1), keys, values)


def attend_kernel(
    chunk, layers,
    facts_ref, start_ref, k_a, v_a, other_ref, msg_ref,
    meta_ref, meta_sem, q_in, q_sem, k_in, v_in, k_sem, v_sem, kc, vc, where_at, vt, qh, scores, peaks, tops, sums, tail,
):
    pages = meta_ref.shape[0]
    load_meta = pltpu.make_async_copy(facts_ref.at[pl.ds(0, pages)], meta_ref, meta_sem)
    load_meta.start()
    pieces, heads, piece, _ = qh.shape
    devices = q_in.shape[0]
    tile = heads * piece
    tokens = pieces * piece
    tokens_here = tokens // devices
    two = 2 * tokens_here
    per_layer = tokens // layers
    first = start_ref[0]
    last = first + tokens - 1
    slot = lax.broadcasted_iota(jnp.int32, (PAGE, HD), 0)
    here = pages // 2

    def fetch(page, keys, values):
        source = pl.ds(lax.rem(page, here) * k_in.shape[1], k_in.shape[1])
        return (
            pltpu.make_async_copy(keys.at[source], k_in.at[page], k_sem.at[page]),
            pltpu.make_async_copy(values.at[source], v_in.at[page], v_sem.at[page]),
        )

    def request(page, keys, values):
        @pl.when(meta_ref[page, 0] <= last)
        def _():
            for copy in fetch(page, keys, values):
                copy.start()

    count = k_a.shape[0]
    k_b, v_b = other_ref.at[pl.ds(0, count)], other_ref.at[pl.ds(count, count)]
    load_q = pltpu.make_async_copy(other_ref.at[pl.ds(2 * count, devices)], q_in, q_sem)
    load_q.start()
    load_meta.wait()
    loop(0, here, lambda p: request(p, k_a, v_a))
    loop(here, pages, lambda p: request(p, k_b, v_b))

    def arrange(chip):
        block = q_in[pl.ds(2 * chip, 2)].astype(F32).reshape(2, heads, tokens_here, HD)
        layer = chip * two // per_layer
        line = layer // pieces * per_layer + lax.rem(chip * two, per_layer)
        target = pl.ds(pl.multiple_of(line, two), two)
        for head in range(heads):
            rows = jnp.concatenate([block[0, head], block[1, head]], axis=0)
            qh[lax.rem(layer, pieces), head, target, :] = rows.astype(BF16)

    def visit(page, used, masked):
        begin, filled = meta_ref[page, 0], meta_ref[page, 1]
        partly = begin + filled - 1 > first
        seen = begin <= last
        take = jnp.logical_and(seen, partly) if masked else jnp.logical_not(partly)

        @pl.when(take)
        def _():
            target = pl.ds(pl.multiple_of(used, 16), PAGE)
            for copy in fetch(page, k_a, v_a):
                copy.wait()
            keys = k_in[page].reshape(PAGE, HD).astype(F32)
            live = slot < filled
            lead = jnp.broadcast_to(keys[0:1, :], (PAGE, HD))
            kc[target, :] = jnp.where(live, keys, lead).astype(BF16)
            tail[...] = lead[0:16, :].astype(BF16)
            vc[target, :] = jnp.where(live, v_in[page].reshape(PAGE, HD).astype(F32), 0.0)
            where_at[target, :] = jnp.where(live, begin + slot, FAR)

        return used + jnp.where(take, (filled + 15) // 16 * 16, 0)

    tail[...] = jnp.zeros_like(tail)
    plain = lax.fori_loop(0, pages, lambda p, u: visit(p, u, False), jnp.int32(0))
    used = lax.fori_loop(0, pages, lambda p, u: visit(p, u, True), plain)
    ending = pl.ds(pl.multiple_of(used, 16), chunk)
    kc[ending, :] = jnp.concatenate([tail[...]] * (chunk // 16), axis=0)
    vc[ending, :] = jnp.zeros((chunk, HD), F32)
    where_at[ending, :] = jnp.full((chunk, HD), FAR, jnp.int32)
    load_q.wait()
    loop(0, devices // 2, arrange)
    chunks = (used + chunk - 1) // chunk
    clear = jnp.where(used > plain, plain // chunk, chunks)
    per_part = SUB // piece
    parts = tile // SUB
    line = lax.broadcasted_iota(jnp.int32, (1, piece), 1)

    def span(position):
        return pl.ds(pl.multiple_of(position * chunk, chunk), chunk)

    def turn_values(position):
        vt[position, 0:HD, :] = vc[span(position), :].T.astype(BF16)
        live = jnp.where(where_at[span(position), :] < FAR, 1.0, 0.0).T
        vt[position, HD : HD + 16, :] = live[0:16, :].astype(BF16)

    def score(tile_index, position, masked, part):
        q = qh[tile_index, part * per_part : (part + 1) * per_part].reshape(SUB, HD)
        s = lax.dot_general(kc[span(position), :], q, (((1,), (1,)), ((), ())), preferred_element_type=F32)
        if masked:
            token = (line // per_layer * pieces + tile_index) * per_layer + lax.rem(line, per_layer)
            seen = where_at[span(position), 0:piece] <= first + token
            s = jnp.concatenate(
                [jnp.where(seen, s[:, head * piece : (head + 1) * piece], NEG) for head in range(per_part)], axis=1
            )
        across = slice(part * SUB, (part + 1) * SUB)
        scores[position, :, across] = s
        peaks[:, across] = jnp.maximum(peaks[:, across], jnp.max(s.reshape(chunk // 8, 8, SUB), axis=0))

    def mix(position, part):
        across = slice(part * SUB, (part + 1) * SUB)
        s = scores[position, :, across].reshape(chunk // 8, 8, SUB)
        weights = jnp.exp2((s - tops[:, across][None]) * LOG2E_SCALE).reshape(chunk, SUB).astype(BF16)
        sums[:, across] += jnp.dot(vt[position], weights, preferred_element_type=F32)

    def settle():
        tops[...] = jnp.broadcast_to(jnp.max(peaks[...], axis=0, keepdims=True), (8, tile))

    sub = lax.broadcasted_iota(jnp.int32, (16, 128), 0)
    blocks = tile // 128

    def finish(tile_index):
        for block in range(blocks):
            across = slice(block * 128, (block + 1) * 128)
            rows = sums[0:HD, across].T.astype(BF16)
            lines = jnp.zeros((16, 128), F32)
            if tile_index:
                lines = msg_ref[0, 2 * block, 64:80, :].astype(F32)
            values = split3(tops[0:1, across] * LOG2E_SCALE) + split3(sums[HD : HD + 1, across])
            for i, value in enumerate(values):
                lines = jnp.where(sub == 6 * tile_index + i, jnp.broadcast_to(value, (16, 128)), lines)
            msg_ref[0, 2 * block, 64:80, :] = lines.astype(BF16)
            turned = jnp.concatenate([lines[:, 64:128], lines[:, 0:64]], axis=1)
            msg_ref[0, 2 * block + 1, 64:80, :] = turned.astype(BF16)
            for part in range(2):
                msg_ref[tile_index, 2 * block + part, 0:64, :] = rows[part * 64 : (part + 1) * 64]

    def grouped(count, step):
        def turn(i):
            for k in range(GROUP):
                step(GROUP * i + k)

        loop(0, count // GROUP, turn)
        loop(count // GROUP * GROUP, count, step)

    def over_chunks(step):
        grouped(clear, lambda c: step(c, False))
        loop(clear, chunks, lambda c: step(c, True))

    def score_all(c, masked):
        turn_values(c)
        for part in range(parts):
            score(0, c, masked, part)

    peaks[...] = jnp.full_like(peaks, NEG)
    over_chunks(score_all)
    settle()

    for t in range(1, pieces):
        peaks[...] = jnp.full_like(peaks, NEG)
        sums[...] = jnp.zeros_like(sums)

        def both(c, masked, t=t):
            for part in range(parts):
                mix(c, part)
                score(t, c, masked, part)

        over_chunks(both)
        finish(t - 1)
        settle()

    def mix_all(c):
        for part in range(parts):
            mix(c, part)

    sums[...] = jnp.zeros_like(sums)
    grouped(chunks, mix_all)
    finish(pieces - 1)


def attend(keys, values, others, meta, start, layers, chunk):
    rows = others.shape[1]
    devices = others.shape[0] - 2 * keys.shape[0]
    pages = 2 * keys.shape[0] * rows // PAGE
    slots = pages * PAGE
    heads = HEADS_HERE // 2
    pieces = 2
    piece = devices * rows // (heads * pieces)
    tile = heads * piece
    dma = pltpu.SemaphoreType.DMA
    vmem = pl.BlockSpec(memory_space=pltpu.VMEM)
    smem = pl.BlockSpec(memory_space=pltpu.SMEM)
    anywhere = pl.BlockSpec(memory_space=pl.ANY)
    return pl.pallas_call(
        functools.partial(attend_kernel, chunk, layers),
        out_shape=jax.ShapeDtypeStruct((pieces, devices // 2, 80, HD), BF16),
        in_specs=[anywhere, smem] + [anywhere] * 3,
        out_specs=vmem,
        scratch_shapes=[
            pltpu.SMEM((pages, 128), jnp.int32),
            dma,
            pltpu.VMEM((devices, rows, HD), BF16),
            dma,
            pltpu.VMEM((pages, PAGE // rows, rows, HD), BF16),
            pltpu.VMEM((pages, PAGE // rows, rows, HD), BF16),
            dma((pages,)),
            dma((pages,)),
            pltpu.VMEM((slots + chunk, HD), BF16),
            pltpu.VMEM((slots + chunk, HD), F32),
            pltpu.VMEM((slots + chunk, HD), jnp.int32),
            pltpu.VMEM((slots // chunk, HD + 16, chunk), BF16),
            pltpu.VMEM((pieces, heads, piece, HD), BF16),
            pltpu.VMEM((slots // chunk, chunk, tile), F32),
            pltpu.VMEM((8, tile), F32),
            pltpu.VMEM((8, tile), F32),
            pltpu.VMEM((HD + 16, tile), F32),
            pltpu.VMEM((16, HD), BF16),
        ],
        compiler_params=pltpu.CompilerParams(vmem_limit_bytes=52 * 1024 * 1024),
        name="attend",
    )(meta, start, keys, values, others)


def split3(row):
    high = row.astype(BF16).astype(F32)
    rest = row - high
    middle = rest.astype(BF16).astype(F32)
    return high, middle, rest - middle


def finish_kernel(
    chips, layers, msg_ref, w_ref, att_ref, z_ref,
    w, in_msg, own_chunk, gathered, natural, terms,
    local_sems, a_send, a_recv, g_send, g_recv, s_send, s_recv, z_send, z_recv,
):
    ctx = lax.axis_index("ctx")
    layer = lax.axis_index("kvh")
    chip, core = ctx // 2, lax.rem(ctx, 2)
    other = {"ctx": ctx + 1 - 2 * core}
    tokens_here, heads, _ = att_ref.shape
    pieces = msg_ref.shape[0]
    _, per_layer, width = z_ref.shape
    half_heads = heads // 2
    depth = half_heads * HD
    piece = chips * 64 // half_heads

    def extent(s):
        return pl.ds(0, 64 if s else 80)

    load_w = pltpu.make_async_copy(w_ref, w, local_sems.at[pieces])
    load_own = [
        pltpu.make_async_copy(msg_ref.at[s, chip, extent(s)], in_msg.at[s, chip, extent(s)], local_sems.at[s])
        for s in range(pieces)
    ]
    peers = [partner(chip, chips, step) for step in steps(chips)]
    far_layers = sorted(range(1, layers), key=lambda k: -min(k, layers - k))
    greet_start(
        [{"ctx": peer * 2 + core} for peer in peers]
        + [{"kvh": lax.rem(layer + k, layers)} for k in far_layers]
        + [other]
    )
    for copy in load_own:
        copy.start()
    load_w.start()
    pl.semaphore_wait(pltpu.get_barrier_semaphore(), chips + layers - 1)

    for s in range(pieces):
        for peer in peers:
            remote(
                msg_ref.at[s, peer, extent(s)], in_msg.at[s, chip, extent(s)], a_send.at[s], a_recv.at[s],
                {"ctx": peer * 2 + core},
            ).start()
    pad = jnp.zeros((128 - chips, 128), F32)
    rest = pl.ds(0, chips - 1)

    def combine(s):
        load_own[s].wait()
        landed(in_msg.at[s, rest, extent(s)], a_recv.at[s])
        tops_in, totals_in = [], []
        for source in range(chips):
            lines = in_msg[0, source, 64:80, :].astype(F32)[6 * s : 6 * s + 6]
            tops_in.append(lines[0:1] + lines[1:2] + lines[2:3])
            totals_in.append(lines[3:4] + lines[4:5] + lines[5:6])
        top = jnp.concatenate(tops_in, axis=0)
        scale = jnp.exp2(top - jnp.max(top, axis=0, keepdims=True))
        total = jnp.sum(scale * jnp.concatenate(totals_in, axis=0), axis=0, keepdims=True)
        turned = jnp.concatenate([scale / total, pad], axis=0).T
        attention = jnp.zeros((64, HD), F32)
        for source in range(chips):
            attention = attention + turned[0:64, source : source + 1] * in_msg[s, source, 0:64, :].astype(F32)
        own_chunk[s] = attention.astype(BF16)
        gathered[s, core, chip] = own_chunk[s]

    def pair_copy(s):
        return remote(gathered.at[s, core], gathered.at[s, core], s_send.at[s], s_recv.at[s], other)

    def product(s, which):
        block = gathered[s, which].reshape(half_heads, piece, HD)
        columns = [block[head] for head in range(half_heads)]
        rows = pl.ds(pl.multiple_of(which * depth, depth), depth)
        return jnp.dot(jnp.concatenate(columns, axis=1), w[rows, :], preferred_element_type=F32)

    for s in range(pieces):
        combine(s)
        for peer in peers:
            remote(
                own_chunk.at[s], gathered.at[s, core, chip], g_send.at[s], g_recv.at[s], {"ctx": peer * 2 + core}
            ).start()
    load_w.wait()
    for s in range(pieces):
        landed(gathered.at[s, core, rest], g_recv.at[s])
        pair_copy(s).start()
        held = product(s, core)
        landed(gathered.at[s, 1 - core], s_recv.at[s])
        ready = (held + product(s, 1 - core)).astype(BF16).reshape(layers // pieces, per_layer, width)
        for j in range(layers // pieces):
            terms[pieces * j + s] = ready[j]
        nearest = layer + lax.rem(layer + s, pieces)
        for k in sorted(range(0, layers, pieces), key=lambda k: -min(k, layers - k)):
            target = lax.rem(nearest + k, layers)

            @pl.when(layer != target)
            def _(target=target):
                remote(terms.at[target], z_ref.at[layer], z_send, z_recv, {"kvh": target}).start()

    keep = pltpu.make_async_copy(terms.at[layer], z_ref.at[layer], local_sems.at[0])
    keep.start()

    two = 2 * tokens_here
    block = chip * two // per_layer
    line = block // pieces * per_layer + lax.rem(chip * two, per_layer)
    for head in range(heads):
        flat = head % half_heads * piece + line
        rows = pl.ds(pl.multiple_of(lax.rem(flat, 64), two), two)
        both = gathered[lax.rem(block, pieces), head // half_heads, flat // 64, rows, :].astype(F32)
        mine = jnp.where(core == 0, both[0:tokens_here], both[tokens_here:two])
        natural[pl.ds(head, tokens_here, stride=heads), :] = mine
    att_ref[...] = natural[...].astype(BF16).reshape(att_ref.shape)

    for s in range(pieces):
        landed(in_msg.at[s, rest, extent(s)], a_send.at[s])
        landed(gathered.at[s, core, rest], g_send.at[s])
        pair_copy(s).wait_send()
    keep.wait()
    layers_rest = z_ref.at[pl.ds(0, layers - 1)]
    landed(layers_rest, z_send)
    landed(layers_rest, z_recv)


def finish(mesh, messages, out_weight, tokens_here):
    chips, layers = mesh.shape["ctx"] // 2, mesh.shape["kvh"]
    width = out_weight.shape[1]
    tokens = chips * 2 * tokens_here
    dma = pltpu.SemaphoreType.DMA
    vmem = pl.BlockSpec(memory_space=pltpu.VMEM)
    anywhere = pl.BlockSpec(memory_space=pl.ANY)
    pieces = messages.shape[0]
    return pl.pallas_call(
        functools.partial(finish_kernel, chips, layers),
        out_shape=(
            jax.ShapeDtypeStruct((tokens_here, HEADS_HERE, HD), BF16),
            jax.ShapeDtypeStruct((layers, tokens // layers, width), BF16),
        ),
        in_specs=[anywhere] * 2,
        out_specs=(vmem, anywhere),
        scratch_shapes=[
            pltpu.VMEM(out_weight.shape, BF16),
            pltpu.VMEM(messages.shape, BF16),
            pltpu.VMEM((pieces, 64, HD), BF16),
            pltpu.VMEM((pieces, 2, chips, 64, HD), BF16),
            pltpu.VMEM((HEADS_HERE * tokens_here, HD), F32),
            pltpu.VMEM((layers, tokens // layers, width), BF16),
            dma((pieces + 1,)),
            dma((pieces,)),
            dma((pieces,)),
            dma((pieces,)),
            dma((pieces,)),
            dma((pieces,)),
            dma((pieces,)),
            dma,
            dma,
        ],
        compiler_params=pltpu.CompilerParams(
            collective_id=1, has_side_effects=True, vmem_limit_bytes=24 * 1024 * 1024
        ),
        name="finish",
    )(messages, out_weight)


def total_kernel(att_ref, z_ref, att_out, proj_out):
    att_out[...] = att_ref[...]
    projected = z_ref[0].astype(F32)
    for source in range(1, z_ref.shape[0]):
        projected = projected + z_ref[source].astype(F32)
    proj_out[...] = projected.astype(BF16)


def total(attention, terms):
    vmem = pl.BlockSpec(memory_space=pltpu.VMEM)
    return pl.pallas_call(
        total_kernel,
        out_shape=(
            jax.ShapeDtypeStruct(attention.shape, BF16),
            jax.ShapeDtypeStruct(terms.shape[1:], BF16),
        ),
        in_specs=[vmem] * 2,
        out_specs=(vmem, vmem),
        compiler_params=pltpu.CompilerParams(vmem_limit_bytes=24 * 1024 * 1024),
        name="total",
    )(attention, terms)


def solution(mesh, chunk=512):
    def local(queries, key_cache, value_cache, block_lengths, block_home, stretch_start, out_weight):
        rows = queries.shape[0] * queries.shape[1] // 2
        keys, values = key_cache.reshape(-1, rows, HD), value_cache.reshape(-1, rows, HD)
        others, meta = gather_queries(mesh, queries, block_lengths, block_home, keys, values)
        messages = attend(keys, values, others, meta, stretch_start, mesh.shape["kvh"], chunk)
        return total(*finish(mesh, messages, out_weight, queries.shape[0]))

    in_specs = (
        P("ctx", "kvh", None),
        P("ctx", "kvh", None),
        P("ctx", "kvh", None),
        P(),
        P(),
        P(),
        P("kvh", "ctx"),
    )
    out_specs = (P("ctx", "kvh", None), P("kvh", "ctx"))
    return jax.shard_map(local, mesh=mesh, in_specs=in_specs, out_specs=out_specs, check_vma=False)
```
